32 devices in a mesh: groups: 2 (over y), row: 4 (over x, core), col: 4 (over z).
Axes of the slice: x: 2, y: 2, z: 4, core: 2. Of those that a mesh axis runs over, the one named last changes fastest.
Arguments:
- density: float32 [8, 4, 1, 8, 4096], P(('groups', 'row'), 'col'), parts along dimension 0, may hold values from -0.84 to 0.84
- density_pattern: int32 [8, 4, 1, 8], P(('groups', 'row'), 'col'), parts along dimension 0, may hold values from -1 to 15, as said below
- response: float32 [8, 4, 1, 8, 4096], P(('groups', 'row'), 'col'), parts along dimension 0, may hold values from -0.84 to 0.84
- response_pattern: int32 [8, 4, 1, 8], P(('groups', 'row'), 'col'), parts along dimension 0, may hold values from -1 to 15, as said below
- density_next_pattern: int32 [8, 4, 1, 8], P(('groups', 'row'), 'col'), parts along dimension 0, may hold values from -1 to 15, as said below
- response_next_pattern: int32 [8, 4, 1, 8], P(('groups', 'row'), 'col'), parts along dimension 0, may hold values from -1 to 15, as said below
- density_out_pattern: int32 [8, 4, 1, 8], P(('groups', 'row'), 'col'), parts along dimension 0, may hold values from -1 to 15, as said below
- response_out_pattern: int32 [8, 4, 1, 8], P(('groups', 'row'), 'col'), parts along dimension 0, may hold values from -1 to 15, as said below
Outputs:
- density_final: float32 [8, 4, 1, 8, 4096], P(('groups', 'row'), 'col'), parts along dimension 0
- response_final: float32 [8, 4, 1, 8, 4096], P(('groups', 'row'), 'col'), parts along dimension 0
The draws below stay inside these ranges and needn't reach their ends.
There are 2 independent parts, one for each index of `groups`. The reference program is written for one: setup_inputs(seed, part) draws one part's arguments, and reference() takes and returns one part's arrays. A program takes and returns all parts, laid end to end along the dimension named above; each array names one. Nothing has to cross between parts.
Inputs may be any that keep to these rules, and one draw needn't show every extreme that they name: `density_pattern`: in every block row the live entries (not -1) are distinct ids of atom groups held by the owning device or by one of its eight neighbours on the periodic 4 x 4 grid of device positions; at least 4 entries of a row are live, and some row has all 8 live. `response_pattern`: as for density_pattern. `density_next_pattern`: as for density_pattern. `response_next_pattern`: as for density_pattern. `density_out_pattern`: as for density_pattern. `response_out_pattern`: as for density_pattern.
All inputs are finite; a program needn't handle non-finite values.
Results may differ from the reference program's by a relative error of at most 0.0003.
Values sent between devices are 32-bit elements; how exact they have to be, the bound alone decides.
No kernel may reach another device: no remote copies, remote signals or barrier semaphores. Data moves between devices by JAX's collectives and lax.ppermute only.
A program may use at most 64 MiB of HBM per device.

```python
import jax
import jax.numpy as jnp
from jax import lax

BLOCK = 64
SLOTS = 8
ROWS_DEV = 1
GRID_ROWS = 4
GRID_COLS = 4
BLOCK_ROWS = 16


def draw_pattern(key):
    grid_rows, grid_cols, per_dev, slot_count = (GRID_ROWS, GRID_COLS, ROWS_DEV, SLOTS)
    key_order, key_dense, key_count, key_full, key_rank = jax.random.split(key, 5)
    row_ids = jnp.arange(grid_rows, dtype=jnp.int32)[:, None, None, None]
    col_ids = jnp.arange(grid_cols, dtype=jnp.int32)[None, :, None, None]
    candidate = jnp.arange(9 * per_dev, dtype=jnp.int32)[None, None, None, :]
    region = candidate // per_dev
    member = candidate % per_dev
    near_row = (row_ids + region // 3 - 1) % grid_rows
    near_col = (col_ids + region % 3 - 1) % grid_cols
    ident = (near_row * grid_cols + near_col) * per_dev + member
    ident = jnp.broadcast_to(ident, (grid_rows, grid_cols, per_dev, 9 * per_dev))
    scores = jax.random.randint(key_order, (grid_rows, grid_cols, per_dev, 9 * per_dev), 0, 1 << 20, dtype=jnp.int32) * (9 * per_dev) + candidate
    order = jnp.argsort(scores, axis=-1)
    chosen = jnp.take_along_axis(ident, order[..., :slot_count], axis=-1)
    dense = jax.random.randint(key_dense, (grid_rows, grid_cols, 1), 0, 2, dtype=jnp.int32)
    lowest = jnp.where(dense == 1, max(slot_count - 3, slot_count // 2), slot_count // 2)
    spread = jax.random.randint(key_count, (grid_rows, grid_cols, per_dev), 0, 1 << 20, dtype=jnp.int32)
    count = spread % (slot_count + 1 - lowest) + lowest
    full_row = jax.random.randint(key_full, (), 0, grid_rows * grid_cols * per_dev, dtype=jnp.int32)
    row_index = jnp.arange(grid_rows * grid_cols * per_dev, dtype=jnp.int32).reshape(grid_rows, grid_cols, per_dev)
    count = jnp.where(row_index == full_row, slot_count, count)
    slot_ids = jnp.arange(slot_count, dtype=jnp.int32)
    rank_scores = jax.random.randint(key_rank, (grid_rows, grid_cols, per_dev, slot_count), 0, 1 << 20, dtype=jnp.int32) * slot_count + slot_ids
    rank = jnp.argsort(jnp.argsort(rank_scores, axis=-1), axis=-1)
    return jnp.where(rank < count[..., None], chosen, -1).astype(jnp.int32)


def draw_density_pattern(key, part):
    key = jax.random.fold_in(key, 11)
    return draw_pattern(key)


def draw_response_pattern(key, part):
    key = jax.random.fold_in(key, 12)
    return draw_pattern(key)


def draw_density_next_pattern(key, part):
    key = jax.random.fold_in(key, 13)
    return draw_pattern(key)


def draw_response_next_pattern(key, part):
    key = jax.random.fold_in(key, 14)
    return draw_pattern(key)


def draw_density_out_pattern(key, part):
    key = jax.random.fold_in(key, 15)
    return draw_pattern(key)


def draw_response_out_pattern(key, part):
    key = jax.random.fold_in(key, 16)
    return draw_pattern(key)


def steps_of(key, extent, pieces, least, top_value):
    def one(position, blocks):
        heights = jax.random.uniform(jax.random.fold_in(jax.random.fold_in(key, 6), position), (blocks,), jnp.float32, least / len(pieces), top_value / len(pieces))
        return jnp.repeat(jnp.exp(heights), extent[position] // blocks).reshape((-1,) + (1,) * (len(extent) - position - 1))

    loudness = one(*pieces[0])
    for cut in pieces[1:]:
        loudness = loudness * one(*cut)
    return loudness


def scatter_about(own_key, extent, scale, most, cuts=(), kind=jnp.bfloat16):
    entries = scale * jax.random.normal(own_key, extent, jnp.float32)
    if cuts:
        entries = entries * steps_of(own_key, extent, cuts, -0.22, 0.18)
    return jnp.clip(entries, -most, most).astype(kind)


def setup_inputs(seed: int = 0, part: int = 0) -> dict:
    keys = jax.random.split(jax.random.key(seed), 9)
    own_keys = jax.random.split(jax.random.fold_in(keys[8], part), 9)
    density = scatter_about(own_keys[0], (GRID_ROWS, GRID_COLS, ROWS_DEV, SLOTS, BLOCK * BLOCK), 0.14, 0.84, ((0, 4), (1, 4)), jnp.float32)
    density_pattern = draw_density_pattern(jax.random.fold_in(jax.random.fold_in(keys[8], part), 71), part)
    response = scatter_about(own_keys[2], (GRID_ROWS, GRID_COLS, ROWS_DEV, SLOTS, BLOCK * BLOCK), 0.14, 0.84, ((0, 4), (1, 4)), jnp.float32)
    response_pattern = draw_response_pattern(jax.random.fold_in(jax.random.fold_in(keys[8], part), 71), part)
    density_next_pattern = draw_density_next_pattern(jax.random.fold_in(jax.random.fold_in(keys[8], part), 71), part)
    response_next_pattern = draw_response_next_pattern(jax.random.fold_in(jax.random.fold_in(keys[8], part), 71), part)
    density_out_pattern = draw_density_out_pattern(jax.random.fold_in(jax.random.fold_in(keys[8], part), 71), part)
    response_out_pattern = draw_response_out_pattern(jax.random.fold_in(jax.random.fold_in(keys[8], part), 71), part)
    return dict(density=density, density_pattern=density_pattern, response=response, response_pattern=response_pattern, density_next_pattern=density_next_pattern, response_next_pattern=response_next_pattern, density_out_pattern=density_out_pattern, response_out_pattern=response_out_pattern)


def carry_over(block_data, pattern, target):
    slot_range = jnp.arange(pattern.shape[-1], dtype=jnp.int32)
    matches = (pattern[..., None, :] == target[..., :, None]) & (target[..., :, None] >= 0)
    located = jnp.any(matches, axis=-1)
    slot_hit = jnp.sum(jnp.where(matches, slot_range, 0), axis=-1).astype(jnp.int32)
    picked = jnp.take_along_axis(block_data, slot_hit[..., None], axis=-2)
    return jnp.where(located[..., None], picked, 0.0)


def block_product(left_data, left_pattern, right_data, right_pattern, target_pattern):
    slot_range = jnp.arange(SLOTS, dtype=jnp.int32)

    def one_row(row_items):
        row_data, row_pattern, row_target = row_items
        live_left = row_pattern >= 0
        source = jnp.where(live_left, row_pattern, 0).astype(jnp.int32)
        right_cols = right_pattern[source]
        matches = (right_cols[:, None, :] == row_target[None, :, None]) & (row_target[None, :, None] >= 0) & live_left[:, None, None]
        located = jnp.any(matches, axis=2)
        slot_hit = jnp.sum(jnp.where(matches, slot_range[None, None, :], 0), axis=2).astype(jnp.int32)
        picked = right_data[source[:, None], slot_hit]
        picked = jnp.where(located[:, :, None], picked, 0.0)
        left_blocks = row_data.reshape(SLOTS, BLOCK, BLOCK)
        right_blocks = picked.reshape(SLOTS, SLOTS, BLOCK, BLOCK)
        result = jnp.einsum("axz,aszy->sxy", left_blocks, right_blocks, precision=lax.Precision.HIGHEST)
        result = result.reshape(SLOTS, BLOCK * BLOCK)
        return jnp.where((row_target >= 0)[:, None], result, 0.0)

    return lax.map(one_row, (left_data, left_pattern, target_pattern))


def reference(density, density_pattern, response, response_pattern, density_next_pattern, response_next_pattern, density_out_pattern, response_out_pattern):
    full_shape = density.shape

    def flat_data(block_data):
        return block_data.reshape(BLOCK_ROWS, SLOTS, BLOCK * BLOCK)

    def flat_pattern(pattern):
        return pattern.reshape(BLOCK_ROWS, SLOTS)

    dens = flat_data(density)
    resp = flat_data(response)
    dens_pat = flat_pattern(density_pattern)
    resp_pat = flat_pattern(response_pattern)
    dnext_pat = flat_pattern(density_next_pattern)
    rnext_pat = flat_pattern(response_next_pattern)
    dout_pat = flat_pattern(density_out_pattern)
    rout_pat = flat_pattern(response_out_pattern)
    density_next = block_product(dens, dens_pat, dens, dens_pat, dnext_pat)
    response_next = block_product(dens, dens_pat, resp, resp_pat, rnext_pat) + block_product(resp, resp_pat, dens, dens_pat, rnext_pat)
    density_final = 2.0 * carry_over(density_next, dnext_pat, dout_pat) - block_product(density_next, dnext_pat, density_next, dnext_pat, dout_pat)
    response_final = 2.0 * carry_over(response_next, rnext_pat, rout_pat) - (block_product(density_next, dnext_pat, response_next, rnext_pat, rout_pat) + block_product(response_next, rnext_pat, density_next, dnext_pat, rout_pat))
    return density_final.reshape(full_shape), response_final.reshape(full_shape)
```

```python
import functools

import jax
import jax.numpy as jnp
from jax import lax
from jax.experimental import pallas as pl
from jax.experimental.pallas import tpu as pltpu
from jax.sharding import PartitionSpec as P

BLOCK = 64
WIDE = 2 * BLOCK
HALF = BLOCK // 2
F32 = jnp.float32
BF16 = jnp.bfloat16
VMEM_LIMIT = 16 * 1024 * 1024


def on_left(rows):
    return lax.broadcasted_iota(jnp.int32, (rows, WIDE), 1) < BLOCK


def swap(tile):
    return pltpu.roll(tile, BLOCK, 1)


def place_of(ident, grid):
    rows, cols = grid
    source = jnp.maximum(ident, 0)
    owner_row = lax.div(source, jnp.int32(cols))
    owner_col = lax.rem(source, jnp.int32(cols))
    down = lax.rem(owner_row - lax.axis_index("row") + 1 + rows, jnp.int32(rows))
    across = lax.rem(owner_col - lax.axis_index("col") + 1 + cols, jnp.int32(cols))
    return jnp.where(ident < 0, 9, down * 3 + across)


def note_slots(pattern, table, grid, slots):
    for place in range(10):
        table[place] = slots
    for slot in range(slots):
        table[place_of(pattern[slot], grid)] = slot


def note_live(pattern, table, grid, slots):
    for place in range(10):
        table[place] = 0
    for slot in range(slots):
        table[place_of(pattern[slot], grid)] = 1


def send_tiles(left, right, to_left, to_right, to_next, to_last, which):
    for e in range(3):
        to_left[e, which] = left[e]
        to_right[e, which] = right[e]
    first = on_left(BLOCK)
    for message, low in ((to_next, 1), (to_last, 0)):
        message[0, which] = left[low]
        message[1, which] = left[low + 1]
        message[2, which] = jnp.where(first, swap(right[low]), right[low + 1])


def spread_kernel(
    grid, slots, first_pattern, second_pattern, first, second, to_left, to_right, to_next, to_last, rows, table
):
    first_half = on_left(HALF)
    even, odd = pl.ds(0, HALF, stride=2), pl.ds(1, HALF, stride=2)
    for which, (pattern, data) in enumerate(((first_pattern, first), (second_pattern, second))):
        note_slots(pattern, table, grid, slots)
        for step in range(HALF):
            rows[which, pl.ds(step, slots, stride=HALF), :] = data[:, step * WIDE : (step + 1) * WIDE]
        rows[which, slots * HALF : (slots + 1) * HALF, :] = jnp.zeros((HALF, WIDE), F32)

        def block(place):
            at = pl.multiple_of(table[place] * HALF, HALF)
            own = rows[which, pl.ds(at, HALF), :]
            return own, swap(own)

        def tile(low, high):
            return (jnp.where(first_half, low[0], high[1]), jnp.where(first_half, low[1], high[0]))

        def put(ref, at, pair):
            ref[at, which, even, :] = pair[0]
            ref[at, which, odd, :] = pair[1]

        last = None
        for e in range(3):
            a, b, c = block(3 * e), block(3 * e + 1), block(3 * e + 2)
            left = tile(a, b)
            put(to_left, e, left)
            put(to_right, e, tile(b, c))
            if e >= 1:
                put(to_next, e - 1, left)
                pair = tile(last, c)
                put(to_next if e == 2 else to_last, 2, pair)
            if e <= 1:
                put(to_last, e, left)
            last = c


def split(tile):
    high = tile.astype(BF16)
    return high, (tile - high.astype(F32)).astype(BF16)


def fill_left_factor(own_left, own_right, factor):
    for side, ref in enumerate((own_left, own_right)):
        for e in range(3):
            at = pl.ds(e * WIDE, WIDE)
            for which, (high_at, low_at) in enumerate(((1, 2), (0, 3))):
                high, low = split(ref[e, which])
                factor[side, high_at * BLOCK : (high_at + 1) * BLOCK, at] = high
                factor[side, low_at * BLOCK : (low_at + 1) * BLOCK, at] = low


def fill_right_factor(
    which, own_left, own_right, from_left, from_right, from_last, from_next, corner_last, corner_next, factor
):
    first = on_left(BLOCK)
    zero = jnp.zeros((BLOCK, WIDE), BF16)

    def put(side, k, e, tile):
        for part, value in enumerate((zero, zero) if tile is None else split(tile)):
            factor[side, part, k * BLOCK : (k + 1) * BLOCK, e * WIDE : (e + 1) * WIDE] = value

    def only_right(tile):
        return jnp.where(first, 0.0, tile)

    for e in range(3):
        put(0, 2, e, from_left[e, which])
        put(0, 3, e, own_left[e, which])
        put(1, 2, e, only_right(own_right[e, which]))
        put(1, 3, e, from_right[e, which])
    for row, own, corner, low in ((0, from_last, corner_last, 0), (2, from_next, corner_next, 1)):
        pack = own[2, which]
        for at in range(2):
            e = low + at
            put(0, 2 * row, e, corner[at, which])
            put(0, 2 * row + 1, e, own[at, which])
            put(1, 2 * row, e, only_right(swap(pack) if at == 0 else pack))
            put(1, 2 * row + 1, e, corner[2 + at, which])
        for side in range(2):
            for k in (2 * row, 2 * row + 1):
                put(side, k, 2 - row, None)


def dot(a, b):
    return lax.dot_general(a, b, (((1,), (0,)), ((), ())), preferred_element_type=F32)


def products(left_factor, right_factor, by_first, by_second):
    sides = []
    for side in range(2):
        a = left_factor[side]
        high = dot(a, by_first[side, 0])
        low = dot(a[: 2 * BLOCK], by_first[side, 1])
        other = dot(a[BLOCK : 3 * BLOCK], by_second[side, 0])
        rest = dot(a[BLOCK : 2 * BLOCK], by_second[side, 1])
        one = high[BLOCK : 2 * BLOCK] + (high[2 * BLOCK : 3 * BLOCK] + low[BLOCK:])
        two = (high[:BLOCK] + (high[3 * BLOCK :] + low[:BLOCK])) + (other[:BLOCK] + (other[BLOCK:] + rest))
        sides.append((one, two))
    first = on_left(BLOCK)
    results = []
    for which in range(2):
        left, right = [], []
        for e in range(3):
            a = sides[0][which][:, e * WIDE : (e + 1) * WIDE]
            b = sides[1][which][:, e * WIDE : (e + 1) * WIDE]
            left.append(a + jnp.where(first, 0.0, swap(b)))
            right.append(b + jnp.where(first, swap(a), 0.0))
        results.append((left, right))
    return results


def multiply(operands, scratch):
    own_left, own_right = operands[:2]
    left_factor, by_first, by_second = scratch
    fill_left_factor(own_left, own_right, left_factor)
    fill_right_factor(0, *operands, by_first)
    fill_right_factor(1, *operands, by_second)
    return products(left_factor, None, by_first, by_second)


def next_kernel(grid, slots, first_pattern, second_pattern, *refs):
    operands, outputs, scratch, table = refs[:8], refs[8:12], refs[12:15], refs[15]
    first = on_left(BLOCK)
    for which, (left, right) in enumerate(multiply(operands, scratch)):
        note_live((first_pattern, second_pattern)[which], table, grid, slots)
        for e in range(3):
            keep_left = jnp.where(first, table[3 * e], table[3 * e + 1]) > 0
            keep_right = jnp.where(first, table[3 * e + 1], table[3 * e + 2]) > 0
            left[e] = jnp.where(keep_left, left[e], 0.0)
            right[e] = jnp.where(keep_right, right[e], 0.0)
        send_tiles(left, right, *outputs, which)


def final_kernel(grid, slots, first_pattern, second_pattern, *refs):
    operands, outputs, scratch, (dense, packed, chosen) = refs[:8], refs[8:10], refs[10:13], refs[13:]
    own_left, own_right = operands[:2]
    first_half = on_left(HALF)
    even, odd = pl.ds(0, HALF, stride=2), pl.ds(1, HALF, stride=2)
    for which, (left, right) in enumerate(multiply(operands, scratch)):
        pattern, out = (first_pattern, second_pattern)[which], outputs[which]
        for e in range(3):
            dense[which, e] = 2.0 * own_left[e, which] - left[e]
            dense[which, 3 + e] = 2.0 * own_right[e, which] - right[e]
        for e in range(3):
            a, b = dense[which, e, even, :], dense[which, e, odd, :]
            packed[which, 3 * e] = jnp.where(first_half, a, swap(b))
            packed[which, 3 * e + 1] = jnp.where(first_half, swap(a), b)
            a, b = dense[which, 3 + e, even, :], dense[which, 3 + e, odd, :]
            packed[which, 3 * e + 2] = jnp.where(first_half, swap(a), b)
        packed[which, 9] = jnp.zeros((HALF, WIDE), F32)
        for slot in range(slots):
            chosen[which, slot * HALF : (slot + 1) * HALF, :] = packed[which, place_of(pattern[slot], grid)]
        for step in range(HALF):
            out[:, step * WIDE : (step + 1) * WIDE] = chosen[which, pl.ds(step, slots, stride=HALF), :]


def shift(block, axis, by):
    count = lax.axis_size(axis)
    return lax.ppermute(block, axis, [(i, (i + by) % count) for i in range(count)])


def exchange(to_left, to_right, to_next, to_last):
    from_left = shift(to_right, "col", 1)
    from_right = shift(to_left, "col", -1)
    from_last = shift(to_next, "row", 1)
    from_next = shift(to_last, "row", -1)
    corner_last = shift(jnp.concatenate([from_left[1:], from_right[1:]]), "row", 1)
    corner_next = shift(jnp.concatenate([from_left[:2], from_right[:2]]), "row", -1)
    return to_left, to_right, from_left, from_right, from_last, from_next, corner_last, corner_next


def shards(
    density,
    density_pattern,
    response,
    response_pattern,
    density_next_pattern,
    response_next_pattern,
    density_out_pattern,
    response_out_pattern,
):
    slots = density.shape[3]
    grid = (lax.axis_size("row"), lax.axis_size("col"))
    smem = pl.BlockSpec(memory_space=pltpu.SMEM)
    vmem = pl.BlockSpec(memory_space=pltpu.VMEM)
    params = pltpu.CompilerParams(vmem_limit_bytes=VMEM_LIMIT)
    message = jax.ShapeDtypeStruct((3, 2, BLOCK, WIDE), F32)
    factors = [
        pltpu.VMEM((2, 4 * BLOCK, 3 * WIDE), BF16),
        pltpu.VMEM((2, 2, 3 * WIDE, 3 * WIDE), BF16),
        pltpu.VMEM((2, 2, 3 * WIDE, 3 * WIDE), BF16),
    ]
    table = pltpu.SMEM((16,), jnp.int32)

    def flat(pattern):
        return pattern.reshape(slots)

    sent = pl.pallas_call(
        functools.partial(spread_kernel, grid, slots),
        out_shape=[message] * 4,
        in_specs=[smem, smem, vmem, vmem],
        out_specs=[vmem] * 4,
        scratch_shapes=[pltpu.VMEM((2, (slots + 1) * HALF, WIDE), F32), table],
        compiler_params=params,
        name="spread",
    )(
        flat(density_pattern),
        flat(response_pattern),
        density.reshape(slots, BLOCK * BLOCK),
        response.reshape(slots, BLOCK * BLOCK),
    )
    sent = pl.pallas_call(
        functools.partial(next_kernel, grid, slots),
        out_shape=[message] * 4,
        in_specs=[smem, smem] + [vmem] * 8,
        out_specs=[vmem] * 4,
        scratch_shapes=factors + [table],
        compiler_params=params,
        name="next_step",
    )(flat(density_next_pattern), flat(response_next_pattern), *exchange(*sent))
    outputs = pl.pallas_call(
        functools.partial(final_kernel, grid, slots),
        out_shape=[jax.ShapeDtypeStruct((slots, BLOCK * BLOCK), F32)] * 2,
        in_specs=[smem, smem] + [vmem] * 8,
        out_specs=[vmem] * 2,
        scratch_shapes=factors
        + [
            pltpu.VMEM((2, 6, BLOCK, WIDE), F32),
            pltpu.VMEM((2, 10, HALF, WIDE), F32),
            pltpu.VMEM((2, slots * HALF, WIDE), F32),
        ],
        compiler_params=params,
        name="final_step",
    )(flat(density_out_pattern), flat(response_out_pattern), *exchange(*sent))
    return tuple(out.reshape(density.shape) for out in outputs)


def solution(mesh):
    data = P(("groups", "row"), "col", None, None, None)
    pattern = P(("groups", "row"), "col", None, None)
    return jax.shard_map(
        shards,
        mesh=mesh,
        in_specs=(data, pattern, data, pattern, pattern, pattern, pattern, pattern),
        out_specs=(data, data),
        check_vma=False,
    )
```

```python
import functools

import jax
import jax.numpy as jnp
from jax import lax
from jax.experimental import pallas as pl
from jax.experimental.pallas import tpu as pltpu
from jax.sharding import PartitionSpec as P

BLOCK = 64
WIDE = 2 * BLOCK
HALF = BLOCK // 2
DEPTH = 3 * BLOCK
F32 = jnp.float32
BF16 = jnp.bfloat16
VMEM_LIMIT = 16 * 1024 * 1024


def on_left(rows):
    return lax.broadcasted_iota(jnp.int32, (rows, WIDE), 1) < BLOCK


def swap(tile):
    return pltpu.roll(tile, BLOCK, 1)


def place_of(ident, grid):
    rows, cols = grid
    source = jnp.maximum(ident, 0)
    owner_row = lax.div(source, jnp.int32(cols))
    owner_col = lax.rem(source, jnp.int32(cols))
    down = lax.rem(owner_row - lax.axis_index("row") + 1 + rows, jnp.int32(rows))
    across = lax.rem(owner_col - lax.axis_index("col") + 1 + cols, jnp.int32(cols))
    return jnp.where(ident < 0, 9, down * 3 + across)


def note_slots(pattern, table, grid, slots):
    for place in range(10):
        table[place] = slots
    for slot in range(slots):
        table[place_of(pattern[0, slot], grid)] = slot


def note_live(pattern, table, grid, slots):
    for place in range(10):
        table[place] = 0
    for slot in range(slots):
        table[place_of(pattern[0, slot], grid)] = 1


def fetch(sources, targets, sems):
    copies = [pltpu.make_async_copy(s, t, sems.at[i]) for i, (s, t) in enumerate(zip(sources, targets))]
    for copy in copies:
        copy.start()
    return copies


def spread_kernel(grid, slots, *refs):
    sources, (to_left, to_right, ask_next, ask_last) = refs[:4], refs[4:8]
    first_pattern, second_pattern, first, second, rows, table, sems = refs[8:]
    copies = fetch(sources, (first_pattern, second_pattern, first, second), sems)
    first_half = on_left(HALF)
    even, odd = pl.ds(0, HALF, stride=2), pl.ds(1, HALF, stride=2)
    for which, (pattern, data) in enumerate(((first_pattern, first), (second_pattern, second))):
        copies[which].wait()
        note_slots(pattern, table, grid, slots)
        rows[which, slots * HALF : (slots + 1) * HALF, :] = jnp.zeros((HALF, WIDE), F32)
        copies[2 + which].wait()
        for step in range(HALF):
            rows[which, pl.ds(step, slots, stride=HALF), :] = data[:, step * WIDE : (step + 1) * WIDE]

        def block(place):
            at = pl.multiple_of(table[place] * HALF, HALF)
            own = rows[which, pl.ds(at, HALF), :]
            return own, swap(own)

        def tile(low, high):
            return (jnp.where(first_half, low[0], high[1]), jnp.where(first_half, low[1], high[0]))

        for e in range(3):
            a, b, c = block(3 * e), block(3 * e + 1), block(3 * e + 2)
            left, right = tile(a, b), tile(b, c)
            for part, stride in enumerate((even, odd)):
                to_left[which, e, stride, :] = left[part]
                to_right[which, e, stride, :] = right[part]
            if e != 1:
                ask = ask_next if e == 2 else ask_last
                for part, stride in enumerate((even, odd)):
                    ask[which, stride, :] = left[part]
                fold_into(ask, which, to_right[which, e])


def fold_into(ask, which, right):
    ask[which, BLOCK:, :] = jnp.where(on_left(HALF), swap(right[:HALF]), right[HALF:])


def split(tile):
    high = tile.astype(BF16)
    return high, (tile - high.astype(F32)).astype(BF16)


HIGH_AT, LOW_AT = (2, 1), (3, 0)


def fill_left_factor(which, left, folded, factor):
    for part, at in ((0, HIGH_AT[which]), (1, LOW_AT[which])):
        factor[at * BLOCK : (at + 1) * BLOCK, :WIDE] = split(left)[part]
        top = split(folded)[part]
        bottom = split(swap(folded))[part]
        factor[at * BLOCK : at * BLOCK + HALF, WIDE:] = top[:, :BLOCK]
        factor[at * BLOCK + HALF : (at + 1) * BLOCK, WIDE:] = bottom[:, :BLOCK]


def fill_right_factor(which, own_left, own_right, from_left, from_right, factor):
    first = on_left(BLOCK)
    zero = jnp.zeros((BLOCK, WIDE), BF16)
    for e in range(3):
        column = e * 2 * WIDE
        tiles = (
            (from_left[which, e], None),
            (own_left[which, e], jnp.where(first, 0.0, own_right[which, e])),
            (None, from_right[which, e]),
        )
        for k, pair in enumerate(tiles):
            for side, tile in enumerate(pair):
                values = (zero, zero) if tile is None else split(tile)
                at = pl.ds(column + side * WIDE, WIDE)
                for part in range(2):
                    factor[part, k * BLOCK : (k + 1) * BLOCK, at] = values[part]


def dot(a, b):
    return lax.dot_general(a, b, (((1,), (0,)), ((), ())), preferred_element_type=F32)


def products(factor, by_first, by_second, low, count):
    at = slice(low * 2 * WIDE, (low + count) * 2 * WIDE)
    high = dot(factor[...], by_first[0, :, at])
    fine = dot(factor[BLOCK : 3 * BLOCK, :], by_first[1, :, at])
    other = dot(factor[2 * BLOCK :, :], by_second[0, :, at])
    rest = dot(factor[2 * BLOCK : 3 * BLOCK, :], by_second[1, :, at])
    one = high[2 * BLOCK : 3 * BLOCK] + (high[3 * BLOCK :] + fine[BLOCK:])
    two = (high[BLOCK : 2 * BLOCK] + (high[:BLOCK] + fine[:BLOCK])) + (other[:BLOCK] + (other[BLOCK:] + rest))
    first = on_left(BLOCK)
    results = []
    for total in (one, two):
        left, right = [], []
        for e in range(count):
            a = total[:, 2 * e * WIDE : (2 * e + 1) * WIDE]
            b = total[:, (2 * e + 1) * WIDE : (2 * e + 2) * WIDE]
            left.append(a + jnp.where(first, 0.0, swap(b)))
            right.append(b)
        results.append((left, right))
    return results


def share_kernel(own_left, own_right, from_left, from_right, from_last, from_next, *refs):
    to_last, to_next, by_first, by_second, factor = refs
    first = on_left(BLOCK)
    for which, by in enumerate((by_first, by_second)):
        fill_right_factor(which, own_left, own_right, from_left, from_right, by)
    for asked, share, low in ((from_last, to_last, 0), (from_next, to_next, 1)):
        for which in range(2):
            fill_left_factor(which, asked[which, :BLOCK], asked[which, BLOCK:], factor)
        for which, (left, right) in enumerate(products(factor, by_first, by_second, low, 2)):
            share[which, 0] = left[0]
            share[which, 1] = left[1]
            share[which, 2] = jnp.where(first, swap(right[0]), right[1])


def own_kernel(own_left, own_right, by_first, by_second, sums, factor):
    for which in range(2):
        right = own_right[which, 1]
        folded = jnp.where(on_left(HALF), swap(right[:HALF]), right[HALF:])
        fill_left_factor(which, own_left[which, 1], folded, factor)
    for which, (left, right) in enumerate(products(factor, by_first, by_second, 0, 3)):
        for e in range(3):
            sums[which, e] = left[e]
            sums[which, 3 + e] = right[e]


def total(which, sums, from_last, from_next):
    left = [sums[which, e] for e in range(3)]
    right = [sums[which, 3 + e] for e in range(3)]
    for share, low in ((from_last, 0), (from_next, 1)):
        left[low] += share[which, 0]
        left[low + 1] += share[which, 1]
        right[low] += swap(share[which, 2])
        right[low + 1] += share[which, 2]
    return left, right


def next_kernel(grid, slots, *refs):
    patterns, (sums, from_last, from_next) = refs[:2], refs[2:5]
    to_left, to_right, ask_next, ask_last = refs[5:9]
    first_pattern, second_pattern, table, sems = refs[9:]
    copies = fetch(patterns, (first_pattern, second_pattern), sems)
    first = on_left(BLOCK)
    for which, pattern in enumerate((first_pattern, second_pattern)):
        left, right = total(which, sums, from_last, from_next)
        copies[which].wait()
        note_live(pattern, table, grid, slots)
        for e in range(3):
            keep = jnp.where(first, table[3 * e], table[3 * e + 1]) > 0
            left_tile = jnp.where(keep, left[e], 0.0)
            right_tile = jnp.where(first, swap(left_tile), jnp.where(table[3 * e + 2] > 0, right[e], 0.0))
            to_left[which, e] = left_tile
            to_right[which, e] = right_tile
            if e != 1:
                ask = ask_next if e == 2 else ask_last
                ask[which, :BLOCK, :] = left_tile
                fold_into(ask, which, right_tile)


def final_kernel(grid, slots, *refs):
    patterns, (own_left, own_right, sums, from_last, from_next), outputs = refs[:2], refs[2:7], refs[7:9]
    first_pattern, second_pattern, dense, packed, chosen, sems = refs[9:]
    copies = fetch(patterns, (first_pattern, second_pattern), sems)
    first_half = on_left(HALF)
    even, odd = pl.ds(0, HALF, stride=2), pl.ds(1, HALF, stride=2)
    for which, pattern in enumerate((first_pattern, second_pattern)):
        out = outputs[which]
        left, right = total(which, sums, from_last, from_next)
        for e in range(3):
            dense[which, e] = 2.0 * own_left[which, e] - left[e]
            dense[which, 3 + e] = 2.0 * own_right[which, e] - right[e]
        for e in range(3):
            a, b = dense[which, e, even, :], dense[which, e, odd, :]
            packed[which, 3 * e] = jnp.where(first_half, a, swap(b))
            packed[which, 3 * e + 1] = jnp.where(first_half, swap(a), b)
            a, b = dense[which, 3 + e, even, :], dense[which, 3 + e, odd, :]
            packed[which, 3 * e + 2] = jnp.where(first_half, swap(a), b)
        packed[which, 9] = jnp.zeros((HALF, WIDE), F32)
        copies[which].wait()
        for slot in range(slots):
            chosen[which, slot * HALF : (slot + 1) * HALF, :] = packed[which, place_of(pattern[0, slot], grid)]
        for step in range(HALF):
            out[:, step * WIDE : (step + 1) * WIDE] = chosen[which, pl.ds(step, slots, stride=HALF), :]


def shift(block, axis, by):
    count = lax.axis_size(axis)
    return lax.ppermute(block, axis, [(i, (i + by) % count) for i in range(count)])


VM = pl.BlockSpec(memory_space=pltpu.VMEM)
HB = pl.BlockSpec(memory_space=pltpu.HBM)
PARAMS = pltpu.CompilerParams(vmem_limit_bytes=VMEM_LIMIT)


def stay(operand):
    return pltpu.with_memory_space_constraint(operand, pltpu.HBM)


def shape(*sizes):
    return jax.ShapeDtypeStruct(sizes, F32)


def multiply(own_left, own_right, ask_next, ask_last):
    from_left = shift(own_right, "col", 1)
    from_right = shift(own_left, "col", -1)
    from_last = shift(ask_next, "row", 1)
    from_next = shift(ask_last, "row", -1)
    by = jax.ShapeDtypeStruct((2, DEPTH, 6 * WIDE), BF16)
    factor = pltpu.VMEM((4 * BLOCK, DEPTH), BF16)
    to_last, to_next, by_first, by_second = pl.pallas_call(
        share_kernel,
        out_shape=[shape(2, 3, BLOCK, WIDE)] * 2 + [by] * 2,
        in_specs=[VM] * 6,
        out_specs=[VM] * 4,
        scratch_shapes=[factor],
        compiler_params=PARAMS,
        name="share",
    )(own_left, own_right, from_left, from_right, from_last, from_next)
    sums = pl.pallas_call(
        own_kernel,
        out_shape=shape(2, 6, BLOCK, WIDE),
        in_specs=[VM] * 4,
        out_specs=VM,
        scratch_shapes=[factor],
        compiler_params=PARAMS,
        cost_estimate=pl.CostEstimate(flops=10**9, bytes_accessed=3 * 10**6, transcendentals=0),
        name="own",
    )(own_left, own_right, by_first, by_second)
    return sums, shift(to_next, "row", 1), shift(to_last, "row", -1)


def shards(
    density,
    density_pattern,
    response,
    response_pattern,
    density_next_pattern,
    response_next_pattern,
    density_out_pattern,
    response_out_pattern,
):
    slots = density.shape[3]
    grid = (lax.axis_size("row"), lax.axis_size("col"))
    pattern = pltpu.SMEM((1, slots), jnp.int32)
    table = pltpu.SMEM((16,), jnp.int32)
    messages = [shape(2, 3, BLOCK, WIDE)] * 2 + [shape(2, BLOCK + HALF, WIDE)] * 2

    def flat(pattern):
        return stay(pattern.reshape(1, slots))

    sent = pl.pallas_call(
        functools.partial(spread_kernel, grid, slots),
        out_shape=messages,
        in_specs=[HB] * 4,
        out_specs=[VM] * 4,
        scratch_shapes=[pattern] * 2
        + [pltpu.VMEM((slots, BLOCK * BLOCK), F32)] * 2
        + [pltpu.VMEM((2, (slots + 1) * HALF, WIDE), F32), table, pltpu.SemaphoreType.DMA((4,))],
        compiler_params=PARAMS,
        name="spread",
    )(
        flat(density_pattern),
        flat(response_pattern),
        stay(density.reshape(slots, BLOCK * BLOCK)),
        stay(response.reshape(slots, BLOCK * BLOCK)),
    )
    sent = pl.pallas_call(
        functools.partial(next_kernel, grid, slots),
        out_shape=messages,
        in_specs=[HB] * 2 + [VM] * 3,
        out_specs=[VM] * 4,
        scratch_shapes=[pattern] * 2 + [table, pltpu.SemaphoreType.DMA((2,))],
        compiler_params=PARAMS,
        name="next_step",
    )(flat(density_next_pattern), flat(response_next_pattern), *multiply(*sent))
    outputs = pl.pallas_call(
        functools.partial(final_kernel, grid, slots),
        out_shape=[shape(slots, BLOCK * BLOCK)] * 2,
        in_specs=[HB] * 2 + [VM] * 5,
        out_specs=[VM] * 2,
        scratch_shapes=[pattern] * 2
        + [
            pltpu.VMEM((2, 6, BLOCK, WIDE), F32),
            pltpu.VMEM((2, 10, HALF, WIDE), F32),
            pltpu.VMEM((2, slots * HALF, WIDE), F32),
            pltpu.SemaphoreType.DMA((2,)),
        ],
        compiler_params=PARAMS,
        name="final_step",
    )(flat(density_out_pattern), flat(response_out_pattern), *sent[:2], *multiply(*sent))
    return tuple(out.reshape(density.shape) for out in outputs)


def solution(mesh):
    data = P(("groups", "row"), "col", None, None, None)
    pattern = P(("groups", "row"), "col", None, None)
    return jax.shard_map(
        shards,
        mesh=mesh,
        in_specs=(data, pattern, data, pattern, pattern, pattern, pattern, pattern),
        out_specs=(data, data),
        check_vma=False,
    )
```

```python
import functools

import jax
import jax.numpy as jnp
from jax import lax
from jax.experimental import pallas as pl
from jax.experimental.pallas import tpu as pltpu
from jax.sharding import PartitionSpec as P

BLOCK = 64
WIDE = 2 * BLOCK
HALF = BLOCK // 2
DEPTH = 3 * BLOCK
ASK_ROWS = BLOCK + HALF
KEEP_ROWS = 8
F32 = jnp.float32
BF16 = jnp.bfloat16
VMEM_LIMIT = 16 * 1024 * 1024


def on_left(rows):
    return lax.broadcasted_iota(jnp.int32, (rows, WIDE), 1) < BLOCK


def swap(tile):
    return pltpu.roll(tile, BLOCK, 1)


def place_of(ident, grid):
    rows, cols = grid
    source = jnp.maximum(ident, 0)
    owner_row = lax.div(source, jnp.int32(cols))
    owner_col = lax.rem(source, jnp.int32(cols))
    down = lax.rem(owner_row - lax.axis_index("row") + 1 + rows, jnp.int32(rows))
    across = lax.rem(owner_col - lax.axis_index("col") + 1 + cols, jnp.int32(cols))
    return jnp.where(ident < 0, 9, down * 3 + across)


def note_slots(pattern, table, grid, slots):
    for place in range(10):
        table[place] = slots
    for slot in range(slots):
        table[place_of(pattern[0, slot], grid)] = slot


def note_live(pattern, table, keep, which, grid, slots):
    for place in range(10):
        table[place] = 0
    for slot in range(slots):
        table[place_of(pattern[0, slot], grid)] = 1
    first = on_left(1)
    for side in range(2):
        for e in range(3):
            low = 3 * e + side
            keep[which, 3 * side + e : 3 * side + e + 1, :] = jnp.where(first, table[low], table[low + 1]).astype(F32)


def fetch(sources, targets, sems):
    copies = [pltpu.make_async_copy(s, t, sems.at[i]) for i, (s, t) in enumerate(zip(sources, targets))]
    for copy in copies:
        copy.start()
    return copies


def spread(slots, grid, pattern, data, to_left, to_right, rows, table, copies):
    first_half = on_left(HALF)
    even, odd = pl.ds(0, HALF, stride=2), pl.ds(1, HALF, stride=2)
    copies[0].wait()
    note_slots(pattern, table, grid, slots)
    rows[slots * HALF : (slots + 1) * HALF, :] = jnp.zeros((HALF, WIDE), F32)
    copies[1].wait()
    for step in range(HALF):
        rows[pl.ds(step, slots, stride=HALF), :] = data[:, step * WIDE : (step + 1) * WIDE]

    def block(place):
        own = rows[pl.ds(pl.multiple_of(table[place] * HALF, HALF), HALF), :]
        return own, swap(own)

    def tile(low, high):
        return (jnp.where(first_half, low[0], high[1]), jnp.where(first_half, low[1], high[0]))

    for e in range(3):
        a, b, c = block(3 * e), block(3 * e + 1), block(3 * e + 2)
        left, right = tile(a, b), tile(b, c)
        for part, stride in enumerate((even, odd)):
            to_left[e, stride, :] = left[part]
            to_right[e, stride, :] = right[part]


def spread_kernel(grid, slots, *refs):
    sources, (first_left, first_right, second_left, second_right, ask_next, ask_last, keep) = refs[:6], refs[6:13]
    patterns, next_patterns, datas, rows, table, sems = refs[13:15], refs[15:17], refs[17:19], *refs[19:]
    copies = fetch(sources, (*patterns, *datas, *next_patterns), sems)
    pairs = ((first_left, first_right), (second_left, second_right))
    for which, pair in enumerate(pairs):
        spread(slots, grid, patterns[which], datas[which], *pair, rows.at[which], table, copies[which :: 2])
    for which, next_pattern in enumerate(next_patterns):
        copies[4 + which].wait()
        note_live(next_pattern, table, keep, which, grid, slots)
    for which, (left, right) in enumerate(pairs):
        at = which * ASK_ROWS
        for ask, e in ((ask_last, 0), (ask_next, 2)):
            ask[at : at + BLOCK, :] = left[e]
            ask[at + BLOCK : at + ASK_ROWS, :] = fold(right[e])
            masks = 2 * ASK_ROWS + KEEP_ROWS * which
            wide = jnp.broadcast_to(keep[which, 3 + e : 4 + e, BLOCK:], (1, BLOCK))
            ask[masks : masks + 1, :] = keep[which, e : e + 1, :]
            ask[masks + 1 : masks + 2, :] = jnp.concatenate([wide, wide], axis=1)
            ask[masks + 2 : masks + KEEP_ROWS, :] = jnp.zeros((KEEP_ROWS - 2, WIDE), F32)


def fold(right):
    return jnp.where(on_left(HALF), swap(right[:HALF]), right[HALF:])


def split(tile):
    high = tile.astype(BF16)
    return high, (tile - high.astype(F32)).astype(BF16)


def fill_left_factor(left, folded, factor):
    for part in range(2):
        at = part * BLOCK
        factor[at : at + BLOCK, :WIDE] = split(left)[part]
        factor[at : at + HALF, WIDE:] = split(folded)[part][:, :BLOCK]
        factor[at + HALF : at + BLOCK, WIDE:] = split(swap(folded))[part][:, :BLOCK]


def fill_right_factor(own_left, own_right, from_left, from_right, factor):
    first = on_left(BLOCK)
    zero = jnp.zeros((BLOCK, WIDE), BF16)
    for e in range(3):
        column = e * 2 * WIDE
        tiles = (
            (from_left[e], None),
            (own_left[e], jnp.where(first, 0.0, own_right[e])),
            (None, from_right[e]),
        )
        for k, pair in enumerate(tiles):
            for side, tile in enumerate(pair):
                values = (zero, zero) if tile is None else split(tile)
                at = pl.ds(column + side * WIDE, WIDE)
                for part in range(2):
                    factor[part, k * BLOCK : (k + 1) * BLOCK, at] = values[part]


def dot(a, b):
    return lax.dot_general(a, b, (((1,), (0,)), ((), ())), preferred_element_type=F32)


def product(factor, by, low, count):
    at = slice(low * 2 * WIDE, (low + count) * 2 * WIDE)
    high = dot(factor[...], by[0, :, at])
    return high[:BLOCK] + (high[BLOCK:] + dot(factor[:BLOCK, :], by[1, :, at]))


def tiles_of(total, count):
    first = on_left(BLOCK)
    left, right = [], []
    for e in range(count):
        a = total[:, 2 * e * WIDE : (2 * e + 1) * WIDE]
        b = total[:, (2 * e + 1) * WIDE : (2 * e + 2) * WIDE]
        left.append(a + jnp.where(first, 0.0, swap(b)))
        right.append(b)
    return left, right


def put_share(total, share):
    left, right = tiles_of(total, 2)
    share[:BLOCK, :] = left[0]
    share[BLOCK:WIDE, :] = left[1]
    share[WIDE:DEPTH, :] = jnp.where(on_left(BLOCK), swap(right[0]), right[1])


def put_sums(total, sums):
    left, right = tiles_of(total, 3)
    for e in range(3):
        sums[e] = left[e]
        sums[3 + e] = right[e]


def put_outer(sums, to_last, to_next):
    for share, e in ((to_last, 0), (to_next, 2)):
        share[DEPTH : DEPTH + BLOCK, :] = sums[e]
        share[DEPTH + BLOCK :, :] = fold(sums[3 + e])


def fill_own(left, right, factor):
    fill_left_factor(left[1], fold(right[1]), factor)


def first_step_first_kernel(own_left, own_right, from_left, from_right, from_last, from_next, *refs):
    to_last, to_next, sums, by, factors = refs
    fill_right_factor(own_left, own_right, from_left, from_right, by)
    for at, (asked, share) in enumerate(((from_last, to_last), (from_next, to_next))):
        factor = factors.at[at]
        fill_left_factor(asked[:BLOCK], asked[BLOCK:ASK_ROWS], factor)
        put_share(product(factor, by, at, 2), share)
    fill_own(own_left, own_right, factors.at[2])
    put_sums(product(factors.at[2], by, 0, 3), sums)
    put_outer(sums, to_last, to_next)


def first_step_second_kernel(own_left, own_right, from_left, from_right, from_last, from_next, *refs):
    first_by, first_factors, to_last, to_next, sums, by, factor = refs
    fill_right_factor(own_left, own_right, from_left, from_right, by)
    for at, (asked, share) in enumerate(((from_last, to_last), (from_next, to_next))):
        fill_left_factor(asked[ASK_ROWS : ASK_ROWS + BLOCK], asked[ASK_ROWS + BLOCK : 2 * ASK_ROWS], factor)
        put_share(product(factor, first_by, at, 2) + product(first_factors.at[at], by, at, 2), share)
    fill_own(own_left, own_right, factor)
    put_sums(product(factor, first_by, 0, 3) + product(first_factors.at[2], by, 0, 3), sums)
    put_outer(sums, to_last, to_next)


def fill_asked(which, masks, received, sent, at, factor):
    pack = sent[WIDE:DEPTH]
    if at == 0:
        left, folded = sent[BLOCK:WIDE], fold(pack)
    else:
        left, folded = sent[:BLOCK], jnp.where(on_left(HALF), pack[:HALF], swap(pack[HALF:]))
    row = 2 * ASK_ROWS + KEEP_ROWS * which
    left = jnp.where(masks[row : row + 1, :] > 0, left + received[DEPTH : DEPTH + BLOCK], 0.0)
    folded = jnp.where(masks[row + 1 : row + 2, :] > 0, folded + received[DEPTH + BLOCK :], 0.0)
    fill_left_factor(left, folded, factor)


def second_step_first_kernel(own_left, own_right, from_left, from_right, *refs):
    asks, received, sent, (to_last, to_next, by, factors) = refs[:2], refs[2:4], refs[4:6], refs[6:]
    fill_right_factor(own_left, own_right, from_left, from_right, by)
    for at, share in enumerate((to_last, to_next)):
        fill_asked(0, asks[at], received[at], sent[at], at, factors.at[at])
        put_share(product(factors.at[at], by, at, 2), share)


def second_step_second_kernel(own_left, own_right, from_left, from_right, *refs):
    asks, received, sent, (first_by, first_factors, to_last, to_next, by, factor) = refs[:2], refs[2:4], refs[4:6], refs[6:]
    fill_right_factor(own_left, own_right, from_left, from_right, by)
    for at, share in enumerate((to_last, to_next)):
        fill_asked(1, asks[at], received[at], sent[at], at, factor)
        put_share(product(factor, first_by, at, 2) + product(first_factors.at[at], by, at, 2), share)


def first_own_kernel(own_left, own_right, by, sums, factor):
    fill_own(own_left, own_right, factor)
    put_sums(product(factor, by, 0, 3), sums)


def second_own_kernel(first_left, first_right, own_left, own_right, first_by, by, sums, factor):
    fill_own(first_left, first_right, factor)
    total = product(factor, by, 0, 3)
    fill_own(own_left, own_right, factor)
    put_sums(total + product(factor, first_by, 0, 3), sums)


def total(sums, from_last, from_next):
    left = [sums[e] for e in range(3)]
    right = [sums[3 + e] for e in range(3)]
    for share, low in ((from_last, 0), (from_next, 1)):
        pack = share[WIDE:DEPTH]
        left[low] += share[:BLOCK]
        left[low + 1] += share[BLOCK:WIDE]
        right[low] += swap(pack)
        right[low + 1] += pack
    return left, right


def next_kernel(which, keep, sums, from_last, from_next, to_left, to_right):
    first = on_left(BLOCK)
    left, right = total(sums, from_last, from_next)
    for e in range(3):
        to_left[e] = jnp.where(keep[which, e : e + 1, :] > 0, left[e], 0.0)
        to_right[e] = jnp.where(keep[which, 3 + e : 4 + e, :] > 0, jnp.where(first, swap(left[e]), right[e]), 0.0)


def final_kernel(grid, slots, pattern_hbm, own_left, own_right, sums, from_last, from_next, _, out, *refs):
    pattern, dense, packed, chosen, sems = refs
    (copy,) = fetch((pattern_hbm,), (pattern,), sems)
    first_half = on_left(HALF)
    even, odd = pl.ds(0, HALF, stride=2), pl.ds(1, HALF, stride=2)
    left, right = total(sums, from_last, from_next)
    for e in range(3):
        dense[e] = 2.0 * own_left[e] - left[e]
        dense[3 + e] = 2.0 * own_right[e] - right[e]
    for e in range(3):
        a, b = dense[e, even, :], dense[e, odd, :]
        packed[3 * e] = jnp.where(first_half, a, swap(b))
        packed[3 * e + 1] = jnp.where(first_half, swap(a), b)
        a, b = dense[3 + e, even, :], dense[3 + e, odd, :]
        packed[3 * e + 2] = jnp.where(first_half, swap(a), b)
    packed[9] = jnp.zeros((HALF, WIDE), F32)
    copy.wait()
    for slot in range(slots):
        chosen[slot * HALF : (slot + 1) * HALF, :] = packed[place_of(pattern[0, slot], grid)]
    for step in range(HALF):
        out[:, step * WIDE : (step + 1) * WIDE] = chosen[pl.ds(step, slots, stride=HALF), :]


def shift(block, axis, by):
    count = lax.axis_size(axis)
    return lax.ppermute(block, axis, [(i, (i + by) % count) for i in range(count)])


VM = pl.BlockSpec(memory_space=pltpu.VMEM)
HB = pl.BlockSpec(memory_space=pltpu.HBM)
PARAMS = pltpu.CompilerParams(vmem_limit_bytes=VMEM_LIMIT)


def stay(operand):
    return pltpu.with_memory_space_constraint(operand, pltpu.HBM)


def shape(*sizes):
    return jax.ShapeDtypeStruct(sizes, F32)


def call(kernel, out_shape, in_specs, out_specs, scratch, name, flops=0):
    return pl.pallas_call(
        kernel,
        out_shape=out_shape,
        in_specs=in_specs,
        out_specs=out_specs,
        scratch_shapes=scratch,
        compiler_params=PARAMS,
        cost_estimate=pl.CostEstimate(flops=flops, bytes_accessed=10**6, transcendentals=0),
        name=name,
    )


TILES = shape(3, BLOCK, WIDE)
ASKS = shape(2 * (ASK_ROWS + KEEP_ROWS), WIDE)
SHARE = shape(DEPTH, WIDE)
LONG_SHARE = shape(DEPTH + ASK_ROWS, WIDE)
SUMS = shape(6, BLOCK, WIDE)
BY = jax.ShapeDtypeStruct((2, DEPTH, 6 * WIDE), BF16)
FACTOR = pltpu.VMEM((WIDE, DEPTH), BF16)


def factors(count):
    return jax.ShapeDtypeStruct((count, WIDE, DEPTH), BF16)


def call_all(kernel, outputs, operands, scratch, name):
    return call(kernel, outputs, [VM] * len(operands), [VM] * len(outputs), scratch, name)(*operands)


def along_col(to_left, to_right):
    return to_left, to_right, shift(to_right, "col", 1), shift(to_left, "col", -1)


def along_row(to_last, to_next):
    return shift(to_next, "row", 1), shift(to_last, "row", -1)


def shards(
    density,
    density_pattern,
    response,
    response_pattern,
    density_next_pattern,
    response_next_pattern,
    density_out_pattern,
    response_out_pattern,
):
    slots = density.shape[3]
    grid = (lax.axis_size("row"), lax.axis_size("col"))
    pattern_scratch = pltpu.SMEM((1, slots), jnp.int32)
    table = pltpu.SMEM((16,), jnp.int32)

    def flat(pattern):
        return stay(pattern.reshape(1, slots))

    def flat_data(data):
        return stay(data.reshape(slots, BLOCK * BLOCK))

    def final_of(pattern, own, parts, earlier):
        scratch = [
            pattern_scratch,
            pltpu.VMEM((6, BLOCK, WIDE), F32),
            pltpu.VMEM((10, HALF, WIDE), F32),
            pltpu.VMEM((slots * HALF, WIDE), F32),
            pltpu.SemaphoreType.DMA((1,)),
        ]
        kernel = functools.partial(final_kernel, grid, slots)
        out = call(kernel, shape(slots, BLOCK * BLOCK), [HB] + [VM] * 5 + [HB], VM, scratch, "final_step")(
            flat(pattern), *own[:2], *parts, stay(earlier)
        )
        return out

    *tiles, ask_next, ask_last, keep = call(
        functools.partial(spread_kernel, grid, slots),
        [TILES] * 4 + [ASKS] * 2 + [shape(2, 8, WIDE)],
        [HB] * 6,
        [VM] * 7,
        [pattern_scratch] * 4
        + [pltpu.VMEM((slots, BLOCK * BLOCK), F32)] * 2
        + [pltpu.VMEM((2, (slots + 1) * HALF, WIDE), F32), table, pltpu.SemaphoreType.DMA((6,))],
        "spread",
    )(
        flat(density_pattern),
        flat(response_pattern),
        flat_data(density),
        flat_data(response),
        flat(density_next_pattern),
        flat(response_next_pattern),
    )

    first = along_col(*tiles[:2])
    asks = along_row(ask_last, ask_next)
    second = along_col(*tiles[2:])
    *first_sent, first_sums, first_by, first_factors = call_all(
        first_step_first_kernel, [LONG_SHARE] * 2 + [SUMS, BY, factors(3)], (*first, *asks), [], "first_share"
    )
    first_got = along_row(*first_sent)
    *second_sent, second_sums = call_all(
        first_step_second_kernel,
        [LONG_SHARE] * 2 + [SUMS],
        (*second, *asks, first_by, first_factors),
        [pltpu.VMEM((2, DEPTH, 6 * WIDE), BF16), FACTOR],
        "second_share",
    )
    second_got = along_row(*second_sent)

    first = along_col(
        *call_all(
            functools.partial(next_kernel, 0), [TILES] * 2, (keep, first_sums, *first_got), [], "first_next"
        )
    )
    second = along_col(
        *call_all(
            functools.partial(next_kernel, 1), [TILES] * 2, (keep, second_sums, *second_got), [], "second_next"
        )
    )
    *first_sent, first_by, first_factors = call_all(
        second_step_first_kernel,
        [SHARE] * 2 + [BY, factors(2)],
        (*first, *asks, *first_got, *first_sent),
        [],
        "first_share",
    )
    first_got = along_row(*first_sent)
    *second_sent, second_by = call_all(
        second_step_second_kernel,
        [SHARE] * 2 + [BY],
        (*second, *asks, *second_got, *second_sent, first_by, first_factors),
        [FACTOR],
        "second_share",
    )
    second_got = along_row(*second_sent)
    (first_sums,) = call_all(first_own_kernel, [SUMS], (*first[:2], first_by), [FACTOR], "first_own")
    (second_sums,) = call_all(
        second_own_kernel, [SUMS], (*first[:2], *second[:2], first_by, second_by), [FACTOR], "second_own"
    )
    first_parts, second_parts = (first_sums, *first_got), (second_sums, *second_got)
    first_out = final_of(density_out_pattern, first, first_parts, flat_data(density))
    second_out = final_of(response_out_pattern, second, second_parts, first_out)
    return first_out.reshape(density.shape), second_out.reshape(density.shape)


def solution(mesh):
    data = P(("groups", "row"), "col", None, None, None)
    pattern = P(("groups", "row"), "col", None, None)
    return jax.shard_map(
        shards,
        mesh=mesh,
        in_specs=(data, pattern, data, pattern, pattern, pattern, pattern, pattern),
        out_specs=(data, data),
        check_vma=False,
    )
```

```python
import functools

import jax
import jax.numpy as jnp
from jax import lax
from jax.experimental import pallas as pl
from jax.experimental.pallas import tpu as pltpu
from jax.sharding import PartitionSpec as P

BLOCK = 64
WIDE = 2 * BLOCK
HALF = BLOCK // 2
DEPTH = 3 * BLOCK
ASK_ROWS = BLOCK + HALF
KEEP_ROWS = 8
PADS = (8, 0, 0, 0, 8, 16, 0, 8)
F32 = jnp.float32
BF16 = jnp.bfloat16
VMEM_LIMIT = 16 * 1024 * 1024


def on_left(rows):
    return lax.broadcasted_iota(jnp.int32, (rows, WIDE), 1) < BLOCK


def swap(tile):
    return pltpu.roll(tile, BLOCK, 1)


def place_of(ident, grid):
    rows, cols = grid
    source = jnp.maximum(ident, 0)
    owner_row = lax.div(source, jnp.int32(cols))
    owner_col = lax.rem(source, jnp.int32(cols))
    down = lax.rem(owner_row - lax.axis_index("row") + 1 + rows, jnp.int32(rows))
    across = lax.rem(owner_col - lax.axis_index("col") + 1 + cols, jnp.int32(cols))
    return jnp.where(ident < 0, 9, down * 3 + across)


def note_slots(pattern, table, grid, slots):
    for place in range(10):
        table[place] = slots
    for slot in range(slots):
        table[place_of(pattern[0, slot], grid)] = slot


def note_live(pattern, table, keep, which, grid, slots):
    for place in range(10):
        table[place] = 0
    for slot in range(slots):
        table[place_of(pattern[0, slot], grid)] = 1
    first = on_left(1)
    for side in range(2):
        for e in range(3):
            low = 3 * e + side
            keep[which, 3 * side + e : 3 * side + e + 1, :] = jnp.where(first, table[low], table[low + 1]).astype(F32)


def tile_at(e):
    return slice(e * BLOCK, (e + 1) * BLOCK)


def fetch(sources, targets, sems):
    copies = [pltpu.make_async_copy(s, t, sems.at[i]) for i, (s, t) in enumerate(zip(sources, targets))]
    for copy in copies:
        copy.start()
    return copies


def fill_rest(message):
    if message.shape[0] > DEPTH:
        message[DEPTH:, :] = jnp.zeros((message.shape[0] - DEPTH, WIDE), F32)


def spread(slots, grid, pattern, data, to_left, to_right, rows, table, copies):
    first_half = on_left(HALF)
    copies[0].wait()
    note_slots(pattern, table, grid, slots)
    rows[slots * HALF : (slots + 1) * HALF, :] = jnp.zeros((HALF, WIDE), F32)
    copies[1].wait()
    for step in range(HALF):
        rows[pl.ds(step, slots, stride=HALF), :] = data[:, step * WIDE : (step + 1) * WIDE]

    def block(place):
        own = rows[pl.ds(pl.multiple_of(table[place] * HALF, HALF), HALF), :]
        return own, swap(own)

    def tile(low, high):
        return (jnp.where(first_half, low[0], high[1]), jnp.where(first_half, low[1], high[0]))

    for e in range(3):
        a, b, c = block(3 * e), block(3 * e + 1), block(3 * e + 2)
        left, right = tile(a, b), tile(b, c)
        for part in range(2):
            to_left[pl.ds(e * BLOCK + part, HALF, stride=2), :] = left[part]
            to_right[pl.ds(e * BLOCK + part, HALF, stride=2), :] = right[part]
    fill_rest(to_left)
    fill_rest(to_right)


def spread_kernel(grid, slots, *refs):
    sources, (first_left, first_right, second_left, second_right, ask_next, ask_last, keep) = refs[:6], refs[6:13]
    patterns, next_patterns, datas, rows, table, sems = refs[13:15], refs[15:17], refs[17:19], *refs[19:]
    copies = fetch(sources, (*patterns, *datas, *next_patterns), sems)
    pairs = ((first_left, first_right), (second_left, second_right))
    for which, pair in enumerate(pairs):
        spread(slots, grid, patterns[which], datas[which], *pair, rows.at[which], table, copies[which :: 2])
    for which, next_pattern in enumerate(next_patterns):
        copies[4 + which].wait()
        note_live(next_pattern, table, keep, which, grid, slots)
    for which, (left, right) in enumerate(pairs):
        at = which * ASK_ROWS
        for ask, e in ((ask_last, 0), (ask_next, 2)):
            ask[at : at + BLOCK, :] = left[tile_at(e)]
            ask[at + BLOCK : at + ASK_ROWS, :] = fold(right[tile_at(e)])
            masks = 2 * ASK_ROWS + KEEP_ROWS * which
            wide = jnp.broadcast_to(keep[which, 3 + e : 4 + e, BLOCK:], (1, BLOCK))
            ask[masks : masks + 1, :] = keep[which, e : e + 1, :]
            ask[masks + 1 : masks + 2, :] = jnp.concatenate([wide, wide], axis=1)
            ask[masks + 2 : masks + KEEP_ROWS, :] = jnp.zeros((KEEP_ROWS - 2, WIDE), F32)


def fold(right):
    return jnp.where(on_left(HALF), swap(right[:HALF]), right[HALF:])


def split(tile):
    high = tile.astype(BF16)
    return high, (tile - high.astype(F32)).astype(BF16)


def fill_left_factor(left, folded, factor):
    for part in range(2):
        at = part * BLOCK
        factor[at : at + BLOCK, :WIDE] = split(left)[part]
        factor[at : at + HALF, WIDE:] = split(folded)[part][:, :BLOCK]
        factor[at + HALF : at + BLOCK, WIDE:] = split(swap(folded))[part][:, :BLOCK]


def fill_right_factor(own_left, own_right, from_left, from_right, factor):
    first = on_left(BLOCK)
    zero = jnp.zeros((BLOCK, WIDE), BF16)
    for e in range(3):
        column = e * 2 * WIDE
        tiles = (
            (from_left[tile_at(e)], None),
            (own_left[tile_at(e)], jnp.where(first, 0.0, own_right[tile_at(e)])),
            (None, from_right[tile_at(e)]),
        )
        for k, pair in enumerate(tiles):
            for side, tile in enumerate(pair):
                values = (zero, zero) if tile is None else split(tile)
                at = pl.ds(column + side * WIDE, WIDE)
                for part in range(2):
                    factor[part, k * BLOCK : (k + 1) * BLOCK, at] = values[part]


def dot(a, b):
    return lax.dot_general(a, b, (((1,), (0,)), ((), ())), preferred_element_type=F32)


def product(factor, by, low, count):
    at = slice(low * 2 * WIDE, (low + count) * 2 * WIDE)
    high = dot(factor[...], by[0, :, at])
    return high[:BLOCK] + (high[BLOCK:] + dot(factor[:BLOCK, :], by[1, :, at]))


def tiles_of(total, count):
    first = on_left(BLOCK)
    left, right = [], []
    for e in range(count):
        a = total[:, 2 * e * WIDE : (2 * e + 1) * WIDE]
        b = total[:, (2 * e + 1) * WIDE : (2 * e + 2) * WIDE]
        left.append(a + jnp.where(first, 0.0, swap(b)))
        right.append(b)
    return left, right


def put_share(total, share):
    left, right = tiles_of(total, 2)
    share[:BLOCK, :] = left[0]
    share[BLOCK:WIDE, :] = left[1]
    share[WIDE:DEPTH, :] = jnp.where(on_left(BLOCK), swap(right[0]), right[1])


def put_sums(total, sums):
    left, right = tiles_of(total, 3)
    for e in range(3):
        sums[e] = left[e]
        sums[3 + e] = right[e]


def put_outer(sums, to_last, to_next):
    for share, e in ((to_last, 0), (to_next, 2)):
        share[DEPTH : DEPTH + BLOCK, :] = sums[e]
        share[DEPTH + BLOCK :, :] = fold(sums[3 + e])


def fill_own(left, right, factor):
    fill_left_factor(left[tile_at(1)], fold(right[tile_at(1)]), factor)


def first_step_first_kernel(own_left, own_right, from_left, from_right, from_last, from_next, *refs):
    to_last, to_next, sums, by, factors = refs
    fill_right_factor(own_left, own_right, from_left, from_right, by)
    for at, (asked, share) in enumerate(((from_last, to_last), (from_next, to_next))):
        factor = factors.at[at]
        fill_left_factor(asked[:BLOCK], asked[BLOCK:ASK_ROWS], factor)
        put_share(product(factor, by, at, 2), share)
    fill_own(own_left, own_right, factors.at[2])
    put_sums(product(factors.at[2], by, 0, 3), sums)
    put_outer(sums, to_last, to_next)


def first_step_second_kernel(own_left, own_right, from_left, from_right, from_last, from_next, *refs):
    first_by, first_factors, to_last, to_next, sums, by, factor = refs
    fill_right_factor(own_left, own_right, from_left, from_right, by)
    for at, (asked, share) in enumerate(((from_last, to_last), (from_next, to_next))):
        fill_left_factor(asked[ASK_ROWS : ASK_ROWS + BLOCK], asked[ASK_ROWS + BLOCK : 2 * ASK_ROWS], factor)
        put_share(product(factor, first_by, at, 2) + product(first_factors.at[at], by, at, 2), share)
    fill_own(own_left, own_right, factor)
    put_sums(product(factor, first_by, 0, 3) + product(first_factors.at[2], by, 0, 3), sums)
    put_outer(sums, to_last, to_next)


def fill_asked(which, masks, received, sent, at, factor):
    pack = sent[WIDE:DEPTH]
    if at == 0:
        left, folded = sent[BLOCK:WIDE], fold(pack)
    else:
        left, folded = sent[:BLOCK], jnp.where(on_left(HALF), pack[:HALF], swap(pack[HALF:]))
    row = 2 * ASK_ROWS + KEEP_ROWS * which
    left = jnp.where(masks[row : row + 1, :] > 0, left + received[DEPTH : DEPTH + BLOCK], 0.0)
    folded = jnp.where(masks[row + 1 : row + 2, :] > 0, folded + received[DEPTH + BLOCK :], 0.0)
    fill_left_factor(left, folded, factor)


def second_step_first_kernel(own_left, own_right, from_left, from_right, *refs):
    asks, received, sent, (to_last, to_next, by, factors) = refs[:2], refs[2:4], refs[4:6], refs[6:]
    fill_right_factor(own_left, own_right, from_left, from_right, by)
    for at, share in enumerate((to_last, to_next)):
        fill_asked(0, asks[at], received[at], sent[at], at, factors.at[at])
        put_share(product(factors.at[at], by, at, 2), share)


def second_step_second_kernel(own_left, own_right, from_left, from_right, *refs):
    asks, received, sent, (first_by, first_factors, to_last, to_next, by, factor) = refs[:2], refs[2:4], refs[4:6], refs[6:]
    fill_right_factor(own_left, own_right, from_left, from_right, by)
    for at, share in enumerate((to_last, to_next)):
        fill_asked(1, asks[at], received[at], sent[at], at, factor)
        put_share(product(factor, first_by, at, 2) + product(first_factors.at[at], by, at, 2), share)


def first_own_kernel(own_left, own_right, by, sums, factor):
    fill_own(own_left, own_right, factor)
    put_sums(product(factor, by, 0, 3), sums)


def second_own_kernel(first_left, first_right, own_left, own_right, first_by, by, sums, factor):
    fill_own(first_left, first_right, factor)
    total = product(factor, by, 0, 3)
    fill_own(own_left, own_right, factor)
    put_sums(total + product(factor, first_by, 0, 3), sums)


def total(sums, from_last, from_next):
    left = [sums[e] for e in range(3)]
    right = [sums[3 + e] for e in range(3)]
    for share, low in ((from_last, 0), (from_next, 1)):
        pack = share[WIDE:DEPTH]
        left[low] += share[:BLOCK]
        left[low + 1] += share[BLOCK:WIDE]
        right[low] += swap(pack)
        right[low + 1] += pack
    return left, right


def next_kernel(which, keep, sums, from_last, from_next, to_left, to_right):
    first = on_left(BLOCK)
    left, right = total(sums, from_last, from_next)
    for e in range(3):
        to_left[tile_at(e), :] = jnp.where(keep[which, e : e + 1, :] > 0, left[e], 0.0)
        right_tile = jnp.where(first, swap(left[e]), right[e])
        to_right[tile_at(e), :] = jnp.where(keep[which, 3 + e : 4 + e, :] > 0, right_tile, 0.0)
    fill_rest(to_left)
    fill_rest(to_right)


def final_kernel(grid, slots, pattern_hbm, own_left, own_right, sums, from_last, from_next, _, out, *refs):
    pattern, dense, packed, chosen, sems = refs
    (copy,) = fetch((pattern_hbm,), (pattern,), sems)
    first_half = on_left(HALF)
    even, odd = pl.ds(0, HALF, stride=2), pl.ds(1, HALF, stride=2)
    left, right = total(sums, from_last, from_next)
    for e in range(3):
        dense[e] = 2.0 * own_left[tile_at(e)] - left[e]
        dense[3 + e] = 2.0 * own_right[tile_at(e)] - right[e]
    for e in range(3):
        a, b = dense[e, even, :], dense[e, odd, :]
        packed[3 * e] = jnp.where(first_half, a, swap(b))
        packed[3 * e + 1] = jnp.where(first_half, swap(a), b)
        a, b = dense[3 + e, even, :], dense[3 + e, odd, :]
        packed[3 * e + 2] = jnp.where(first_half, swap(a), b)
    packed[9] = jnp.zeros((HALF, WIDE), F32)
    copy.wait()
    for slot in range(slots):
        chosen[slot * HALF : (slot + 1) * HALF, :] = packed[place_of(pattern[0, slot], grid)]
    for step in range(HALF):
        out[:, step * WIDE : (step + 1) * WIDE] = chosen[pl.ds(step, slots, stride=HALF), :]


def shift(block, axis, by):
    count = lax.axis_size(axis)
    return lax.ppermute(block, axis, [(i, (i + by) % count) for i in range(count)])


VM = pl.BlockSpec(memory_space=pltpu.VMEM)
HB = pl.BlockSpec(memory_space=pltpu.HBM)
PARAMS = pltpu.CompilerParams(vmem_limit_bytes=VMEM_LIMIT)


def stay(operand):
    return pltpu.with_memory_space_constraint(operand, pltpu.HBM)


def shape(*sizes):
    return jax.ShapeDtypeStruct(sizes, F32)


def call(kernel, out_shape, in_specs, out_specs, scratch, name, flops=0):
    return pl.pallas_call(
        kernel,
        out_shape=out_shape,
        in_specs=in_specs,
        out_specs=out_specs,
        scratch_shapes=scratch,
        compiler_params=PARAMS,
        cost_estimate=pl.CostEstimate(flops=flops, bytes_accessed=10**6, transcendentals=0),
        name=name,
    )


def tiles_shape(rest):
    return shape(DEPTH + rest, WIDE)


ASKS = shape(2 * (ASK_ROWS + KEEP_ROWS), WIDE)
SHARE = shape(DEPTH, WIDE)
LONG_SHARE = shape(DEPTH + ASK_ROWS, WIDE)
SUMS = shape(6, BLOCK, WIDE)
BY = jax.ShapeDtypeStruct((2, DEPTH, 6 * WIDE), BF16)
FACTOR = pltpu.VMEM((WIDE, DEPTH), BF16)


def factors(count):
    return jax.ShapeDtypeStruct((count, WIDE, DEPTH), BF16)


def call_all(kernel, outputs, operands, scratch, name):
    return call(kernel, outputs, [VM] * len(operands), [VM] * len(outputs), scratch, name)(*operands)


def along_col(to_left, to_right):
    return to_left, to_right, shift(to_right, "col", 1), shift(to_left, "col", -1)


def along_row(to_last, to_next):
    return shift(to_next, "row", 1), shift(to_last, "row", -1)


def shards(
    density,
    density_pattern,
    response,
    response_pattern,
    density_next_pattern,
    response_next_pattern,
    density_out_pattern,
    response_out_pattern,
):
    slots = density.shape[3]
    grid = (lax.axis_size("row"), lax.axis_size("col"))
    pattern_scratch = pltpu.SMEM((1, slots), jnp.int32)
    table = pltpu.SMEM((16,), jnp.int32)

    def flat(pattern):
        return stay(pattern.reshape(1, slots))

    def flat_data(data):
        return stay(data.reshape(slots, BLOCK * BLOCK))

    def final_of(pattern, own, parts, earlier):
        scratch = [
            pattern_scratch,
            pltpu.VMEM((6, BLOCK, WIDE), F32),
            pltpu.VMEM((10, HALF, WIDE), F32),
            pltpu.VMEM((slots * HALF, WIDE), F32),
            pltpu.SemaphoreType.DMA((1,)),
        ]
        kernel = functools.partial(final_kernel, grid, slots)
        out = call(kernel, shape(slots, BLOCK * BLOCK), [HB] + [VM] * 5 + [HB], VM, scratch, "final_step")(
            flat(pattern), *own[:2], *parts, stay(earlier)
        )
        return out

    *tiles, ask_next, ask_last, keep = call(
        functools.partial(spread_kernel, grid, slots),
        [tiles_shape(r) for r in PADS[:4]] + [ASKS] * 2 + [shape(2, 8, WIDE)],
        [HB] * 6,
        [VM] * 7,
        [pattern_scratch] * 4
        + [pltpu.VMEM((slots, BLOCK * BLOCK), F32)] * 2
        + [pltpu.VMEM((2, (slots + 1) * HALF, WIDE), F32), table, pltpu.SemaphoreType.DMA((6,))],
        "spread",
    )(
        flat(density_pattern),
        flat(response_pattern),
        flat_data(density),
        flat_data(response),
        flat(density_next_pattern),
        flat(response_next_pattern),
    )

    first = along_col(*tiles[:2])
    asks = along_row(ask_last, ask_next)
    second = along_col(*tiles[2:])
    *first_sent, first_sums, first_by, first_factors = call_all(
        first_step_first_kernel, [LONG_SHARE] * 2 + [SUMS, BY, factors(3)], (*first, *asks), [], "first_share"
    )
    first_got = along_row(*first_sent)
    *second_sent, second_sums = call_all(
        first_step_second_kernel,
        [LONG_SHARE] * 2 + [SUMS],
        (*second, *asks, first_by, first_factors),
        [pltpu.VMEM((2, DEPTH, 6 * WIDE), BF16), FACTOR],
        "second_share",
    )
    second_got = along_row(*second_sent)

    first = along_col(
        *call_all(
            functools.partial(next_kernel, 0), [tiles_shape(r) for r in PADS[4:6]], (keep, first_sums, *first_got), [], "first_next"
        )
    )
    second = along_col(
        *call_all(
            functools.partial(next_kernel, 1), [tiles_shape(r) for r in PADS[6:8]], (keep, second_sums, *second_got), [], "second_next"
        )
    )
    *first_sent, first_by, first_factors = call_all(
        second_step_first_kernel,
        [SHARE] * 2 + [BY, factors(2)],
        (*first, *asks, *first_got, *first_sent),
        [],
        "first_share",
    )
    first_got = along_row(*first_sent)
    *second_sent, second_by = call_all(
        second_step_second_kernel,
        [SHARE] * 2 + [BY],
        (*second, *asks, *second_got, *second_sent, first_by, first_factors),
        [FACTOR],
        "second_share",
    )
    second_got = along_row(*second_sent)
    (first_sums,) = call_all(first_own_kernel, [SUMS], (*first[:2], first_by), [FACTOR], "first_own")
    (second_sums,) = call_all(
        second_own_kernel, [SUMS], (*first[:2], *second[:2], first_by, second_by), [FACTOR], "second_own"
    )
    first_parts, second_parts = (first_sums, *first_got), (second_sums, *second_got)
    first_out = final_of(density_out_pattern, first, first_parts, flat_data(density))
    second_out = final_of(response_out_pattern, second, second_parts, first_out)
    return first_out.reshape(density.shape), second_out.reshape(density.shape)


def solution(mesh):
    data = P(("groups", "row"), "col", None, None, None)
    pattern = P(("groups", "row"), "col", None, None)
    return jax.shard_map(
        shards,
        mesh=mesh,
        in_specs=(data, pattern, data, pattern, pattern, pattern, pattern, pattern),
        out_specs=(data, data),
        check_vma=False,
    )
```

```python
import functools

import jax
import jax.numpy as jnp
from jax import lax
from jax.experimental import pallas as pl
from jax.experimental.pallas import tpu as pltpu
from jax.sharding import PartitionSpec as P

BLOCK = 64
WIDE = 2 * BLOCK
HALF = BLOCK // 2
DEPTH = 3 * BLOCK
ASK_ROWS = BLOCK + HALF
PADS = (16, 8, 0, 0, 8, 16, 0, 8)
F32 = jnp.float32
BF16 = jnp.bfloat16
VMEM_LIMIT = 16 * 1024 * 1024


def on_left(rows):
    return lax.broadcasted_iota(jnp.int32, (rows, WIDE), 1) < BLOCK


def swap(tile):
    return pltpu.roll(tile, BLOCK, 1)


def place_of(ident, grid):
    rows, cols = grid
    source = jnp.maximum(ident, 0)
    owner_row = lax.div(source, jnp.int32(cols))
    owner_col = lax.rem(source, jnp.int32(cols))
    down = lax.rem(owner_row - lax.axis_index("row") + 1 + rows, jnp.int32(rows))
    across = lax.rem(owner_col - lax.axis_index("col") + 1 + cols, jnp.int32(cols))
    return jnp.where(ident < 0, 9, down * 3 + across)


def note_slots(pattern, table, grid, slots):
    for place in range(10):
        table[place] = slots
    for slot in range(slots):
        table[place_of(pattern[0, slot], grid)] = slot


def ident_at(place, grid):
    rows, cols = grid
    row = lax.rem(lax.axis_index("row") + place // 3 - 1 + rows, jnp.int32(rows))
    col = lax.rem(lax.axis_index("col") + place % 3 - 1 + cols, jnp.int32(cols))
    return (row * cols + col).astype(F32)


def pair_at(low, high, grid):
    return jnp.where(on_left(1), ident_at(low, grid), ident_at(high, grid))


def is_live(idents, wanted):
    return jnp.max(jnp.where(idents == wanted, 1.0, 0.0), axis=0, keepdims=True) > 0


def tile_at(e):
    return slice(e * BLOCK, (e + 1) * BLOCK)


def fetch(sources, targets, sems):
    copies = [pltpu.make_async_copy(s, t, sems.at[i]) for i, (s, t) in enumerate(zip(sources, targets))]
    for copy in copies:
        copy.start()
    return copies


def fill_rest(message):
    if message.shape[0] > DEPTH:
        message[DEPTH:, :] = jnp.zeros((message.shape[0] - DEPTH, WIDE), F32)


def spread(slots, grid, pattern, data, to_left, to_right, rows, table, copies):
    first_half = on_left(HALF)
    copies[0].wait()
    note_slots(pattern, table, grid, slots)
    rows[slots * HALF : (slots + 1) * HALF, :] = jnp.zeros((HALF, WIDE), F32)
    copies[1].wait()
    for step in range(HALF):
        rows[pl.ds(step, slots, stride=HALF), :] = data[:, step * WIDE : (step + 1) * WIDE]

    def block(place):
        own = rows[pl.ds(pl.multiple_of(table[place] * HALF, HALF), HALF), :]
        return own, swap(own)

    def tile(low, high):
        return (jnp.where(first_half, low[0], high[1]), jnp.where(first_half, low[1], high[0]))

    for e in range(3):
        a, b, c = block(3 * e), block(3 * e + 1), block(3 * e + 2)
        left, right = tile(a, b), tile(b, c)
        for part in range(2):
            to_left[pl.ds(e * BLOCK + part, HALF, stride=2), :] = left[part]
            to_right[pl.ds(e * BLOCK + part, HALF, stride=2), :] = right[part]
    fill_rest(to_left)
    fill_rest(to_right)


def spread_kernel(grid, slots, *refs):
    sources, (first_left, first_right, second_left, second_right, idents) = refs[:8], refs[8:13]
    patterns, datas, later, (rows, table, sems) = refs[13:15], refs[15:17], refs[17:21], refs[21:]
    copies = fetch(sources, (*patterns, *datas, *later), sems)
    pairs = ((first_left, first_right), (second_left, second_right))
    for which, pair in enumerate(pairs):
        spread(slots, grid, patterns[which], datas[which], *pair, rows.at[which], table, copies[which :: 2])
    for which, pattern in enumerate(later):
        copies[4 + which].wait()
        for slot in range(slots):
            idents[which, slot : slot + 1, :] = jnp.full((1, WIDE), pattern[0, slot].astype(F32), F32)


def ask_kernel(slots, first_left, first_right, second_left, second_right, idents, ask_last, ask_next):
    for which, (left, right) in enumerate(((first_left, first_right), (second_left, second_right))):
        at = which * ASK_ROWS
        for ask, e in ((ask_last, 0), (ask_next, 2)):
            ask[at : at + BLOCK, :] = left[tile_at(e)]
            ask[at + BLOCK : at + ASK_ROWS, :] = fold(right[tile_at(e)])
            masks = 2 * ASK_ROWS + slots * which
            ask[masks : masks + slots, :] = idents[which]


def fold(right):
    return jnp.where(on_left(HALF), swap(right[:HALF]), right[HALF:])


def split(tile):
    high = tile.astype(BF16)
    return high, (tile - high.astype(F32)).astype(BF16)


def put_depth(factor, rows, tile):
    high, low = split(tile)
    for part, value in enumerate((high, low, high)):
        factor[rows, part * WIDE : (part + 1) * WIDE] = value


def fill_left_factor(at, left, right, factor):
    rows = tile_at(at)
    put_depth(factor.at[0], rows, left)
    put_depth(factor.at[1], rows, right)


def unfold(left, folded):
    first = on_left(HALF)
    other = jnp.concatenate([jnp.where(first, folded, swap(folded)), jnp.where(first, swap(folded), folded)], axis=0)
    return jnp.where(on_left(BLOCK), swap(left), other)


def fill_right_factor(own_left, own_right, from_left, from_right, factor):
    first = on_left(BLOCK)
    for e in range(3):
        at = pl.ds(e * WIDE, WIDE)
        near = jnp.where(first, 0.0, own_right[tile_at(e)])
        for side, pair in enumerate(((from_left[tile_at(e)], own_left[tile_at(e)]), (near, from_right[tile_at(e)]))):
            for k, tile in enumerate(pair):
                high, low = split(tile)
                for part, value in enumerate((high, high, low)):
                    factor[side, tile_at(2 * part + k), at] = value


def product(factor, by):
    return [
        lax.dot_general(factor[side], by[side], (((1,), (0,)), ((), ())), preferred_element_type=F32)
        for side in range(2)
    ]


def tiles_of(total, at, low, count):
    first = on_left(BLOCK)
    left, right = [], []
    for e in range(low, low + count):
        a, b = (side[tile_at(at), e * WIDE : (e + 1) * WIDE] for side in total)
        left.append(a + jnp.where(first, 0.0, swap(b)))
        right.append(b)
    return left, right


def put_all(total, to_last, to_next, sums):
    for at, low, share in ((0, 0, to_last), (1, 1, to_next)):
        left, right = tiles_of(total, at, low, 2)
        share[:BLOCK, :] = left[0]
        share[BLOCK:WIDE, :] = left[1]
        share[WIDE:DEPTH, :] = jnp.where(on_left(BLOCK), swap(right[0]), right[1])
    left, right = tiles_of(total, 2, 0, 3)
    for e in range(3):
        sums[e] = left[e]
        sums[3 + e] = right[e]
    for share, e in ((to_last, 0), (to_next, 2)):
        if share.shape[0] > DEPTH:
            share[DEPTH : DEPTH + BLOCK, :] = left[e]
            share[DEPTH + BLOCK :, :] = fold(right[e])


def fill_own(left, right, factor):
    fill_left_factor(2, left[tile_at(1)], right[tile_at(1)], factor)


def fill_asked(which, grid, slots, asks, got, sent, factor):
    for at in range(2):
        if got is None:
            row = which * ASK_ROWS
            left, folded = asks[at][row : row + BLOCK], asks[at][row + BLOCK : row + ASK_ROWS]
        else:
            pack = sent[at][WIDE:DEPTH]
            if at == 0:
                left, folded = sent[at][BLOCK:WIDE], fold(pack)
            else:
                left, folded = sent[at][:BLOCK], jnp.where(on_left(HALF), pack[:HALF], swap(pack[HALF:]))
            row = 2 * ASK_ROWS + slots * which
            idents = asks[at][row : row + slots]
            left = jnp.where(is_live(idents, pair_at(3, 4, grid)), left + got[at][DEPTH : DEPTH + BLOCK], 0.0)
            folded = jnp.where(is_live(idents, ident_at(5, grid)), folded + got[at][DEPTH + BLOCK :], 0.0)
        fill_left_factor(at, left, unfold(left, folded), factor)


def first_share_kernel(grid, slots, earlier, *refs):
    tiles, asks, refs = refs[:4], refs[4:6], refs[6:]
    got, sent = (refs[:2], refs[2:4]) if earlier else (None, None)
    to_last, to_next, sums, by, factor = refs[4 if earlier else 0 :]
    fill_right_factor(*tiles, by)
    fill_asked(0, grid, slots, asks, got, sent, factor)
    fill_own(tiles[0], tiles[1], factor)
    put_all(product(factor, by), to_last, to_next, sums)


def second_share_kernel(grid, slots, earlier, *refs):
    tiles, asks, refs = refs[:4], refs[4:6], refs[6:]
    got, sent = (refs[:2], refs[2:4]) if earlier else (None, None)
    first_by, first_factor, to_last, to_next, sums, by, factor = refs[4 if earlier else 0 :]
    fill_right_factor(*tiles, by)
    fill_asked(1, grid, slots, asks, got, sent, factor)
    fill_own(tiles[0], tiles[1], factor)
    both = [a + b for a, b in zip(product(factor, first_by), product(first_factor, by))]
    put_all(both, to_last, to_next, sums)


def total(sums, from_last, from_next):
    left = [sums[e] for e in range(3)]
    right = [sums[3 + e] for e in range(3)]
    for share, low in ((from_last, 0), (from_next, 1)):
        pack = share[WIDE:DEPTH]
        left[low] += share[:BLOCK]
        left[low + 1] += share[BLOCK:WIDE]
        right[low] += swap(pack)
        right[low + 1] += pack
    return left, right


def next_kernel(which, grid, idents, sums, from_last, from_next, to_left, to_right):
    first = on_left(BLOCK)
    left, right = total(sums, from_last, from_next)
    for e in range(3):
        keep_left = is_live(idents[which], pair_at(3 * e, 3 * e + 1, grid))
        keep_right = is_live(idents[which], pair_at(3 * e + 1, 3 * e + 2, grid))
        to_left[tile_at(e), :] = jnp.where(keep_left, left[e], 0.0)
        to_right[tile_at(e), :] = jnp.where(keep_right, jnp.where(first, swap(left[e]), right[e]), 0.0)
    fill_rest(to_left)
    fill_rest(to_right)


def final_kernel(which, grid, slots, idents, own_left, own_right, sums, from_last, from_next, _, out, dense, packed):
    first_half = on_left(HALF)
    even, odd = pl.ds(0, HALF, stride=2), pl.ds(1, HALF, stride=2)
    left, right = total(sums, from_last, from_next)
    for e in range(3):
        dense[e] = 2.0 * own_left[tile_at(e)] - left[e]
        dense[3 + e] = 2.0 * own_right[tile_at(e)] - right[e]
    for e in range(3):
        a, b = dense[e, even, :], dense[e, odd, :]
        packed[3 * e] = jnp.where(first_half, a, swap(b))
        packed[3 * e + 1] = jnp.where(first_half, swap(a), b)
        a, b = dense[3 + e, even, :], dense[3 + e, odd, :]
        packed[3 * e + 2] = jnp.where(first_half, swap(a), b)
    slot_holds = [idents[2 + which] == ident_at(place, grid) for place in range(9)]
    for step in range(HALF):
        line = jnp.zeros((slots, WIDE), F32)
        for place in range(9):
            line = jnp.where(slot_holds[place], packed[place, step : step + 1, :], line)
        out[:, step * WIDE : (step + 1) * WIDE] = line


def shift(block, axis, by):
    count = lax.axis_size(axis)
    return lax.ppermute(block, axis, [(i, (i + by) % count) for i in range(count)])


VM = pl.BlockSpec(memory_space=pltpu.VMEM)
HB = pl.BlockSpec(memory_space=pltpu.HBM)
PARAMS = pltpu.CompilerParams(vmem_limit_bytes=VMEM_LIMIT)


def stay(operand):
    return pltpu.with_memory_space_constraint(operand, pltpu.HBM)


def shape(*sizes):
    return jax.ShapeDtypeStruct(sizes, F32)


def call(kernel, out_shape, in_specs, out_specs, scratch, name, flops=0):
    return pl.pallas_call(
        kernel,
        out_shape=out_shape,
        in_specs=in_specs,
        out_specs=out_specs,
        scratch_shapes=scratch,
        compiler_params=PARAMS,
        cost_estimate=pl.CostEstimate(flops=flops, bytes_accessed=10**6, transcendentals=0),
        name=name,
    )


def tiles_shape(rest):
    return shape(DEPTH + rest, WIDE)


SHARE = shape(DEPTH, WIDE)
LONG_SHARE = shape(DEPTH + ASK_ROWS, WIDE)
SUMS = shape(6, BLOCK, WIDE)
BY_SHAPE = (2, 3 * WIDE, 3 * WIDE)
FACTOR_SHAPE = (2, 3 * BLOCK, 3 * WIDE)


def call_all(kernel, outputs, operands, scratch, name):
    return call(kernel, outputs, [VM] * len(operands), [VM] * len(outputs), scratch, name)(*operands)


def along_col(to_left, to_right):
    return to_left, to_right, shift(to_right, "col", 1), shift(to_left, "col", -1)


def along_row(to_last, to_next):
    return shift(to_next, "row", 1), shift(to_last, "row", -1)


def shards(
    density,
    density_pattern,
    response,
    response_pattern,
    density_next_pattern,
    response_next_pattern,
    density_out_pattern,
    response_out_pattern,
):
    slots = density.shape[3]
    grid = (lax.axis_size("row"), lax.axis_size("col"))
    pattern_scratch = pltpu.SMEM((1, slots), jnp.int32)
    table = pltpu.SMEM((16,), jnp.int32)

    def flat(pattern):
        return stay(pattern.reshape(1, slots))

    def flat_data(data):
        return stay(data.reshape(slots, BLOCK * BLOCK))

    *tiles, idents = call(
        functools.partial(spread_kernel, grid, slots),
        [tiles_shape(r) for r in PADS[:4]] + [shape(4, slots, WIDE)],
        [HB] * 8,
        [VM] * 5,
        [pattern_scratch] * 2
        + [pltpu.VMEM((slots, BLOCK * BLOCK), F32)] * 2
        + [pattern_scratch] * 4
        + [pltpu.VMEM((2, (slots + 1) * HALF, WIDE), F32), table, pltpu.SemaphoreType.DMA((8,))],
        "spread",
    )(
        flat(density_pattern),
        flat(response_pattern),
        flat_data(density),
        flat_data(response),
        flat(density_next_pattern),
        flat(response_next_pattern),
        flat(density_out_pattern),
        flat(response_out_pattern),
    )

    def share(first, second, asks, shape_of_share, earlier):
        outputs = [shape_of_share] * 2 + [SUMS]
        factors = [jax.ShapeDtypeStruct(BY_SHAPE, BF16), jax.ShapeDtypeStruct(FACTOR_SHAPE, BF16)]
        scratch = [pltpu.VMEM(BY_SHAPE, BF16), pltpu.VMEM(FACTOR_SHAPE, BF16)]
        *first_sent, first_sums, first_by, first_factor = call_all(
            functools.partial(first_share_kernel, grid, slots, bool(earlier)),
            outputs + factors,
            (*first, *asks, *(earlier[0] if earlier else ())),
            [],
            "first_share",
        )
        first_got = along_row(*first_sent)
        *second_sent, second_sums = call_all(
            functools.partial(second_share_kernel, grid, slots, bool(earlier)),
            outputs,
            (*second, *asks, *(earlier[1] if earlier else ()), first_by, first_factor),
            scratch,
            "second_share",
        )
        second_got = along_row(*second_sent)
        return (first_sums, *first_got), (second_sums, *second_got), first_sent, second_sent

    first = along_col(*tiles[:2])
    asks = along_row(
        *call_all(
            functools.partial(ask_kernel, slots),
            [shape(2 * (ASK_ROWS + slots), WIDE)] * 2,
            (*tiles, idents),
            [],
            "ask",
        )
    )
    second = along_col(*tiles[2:])
    first_parts, second_parts, first_sent, second_sent = share(first, second, asks, LONG_SHARE, ())
    earlier = ((*first_parts[1:], *first_sent), (*second_parts[1:], *second_sent))
    next_tiles = [
        call_all(
            functools.partial(next_kernel, which, grid),
            [tiles_shape(r) for r in PADS[4 + 2 * which : 6 + 2 * which]],
            (idents, *parts),
            [],
            name,
        )
        for which, parts, name in ((0, first_parts, "first_next"), (1, second_parts, "second_next"))
    ]
    first, second = along_col(*next_tiles[0]), along_col(*next_tiles[1])
    first_parts, second_parts, _, _ = share(first, second, asks, SHARE, earlier)

    def final_of(which, own, parts, earlier, name):
        scratch = [pltpu.VMEM((6, BLOCK, WIDE), F32), pltpu.VMEM((9, HALF, WIDE), F32)]
        kernel = functools.partial(final_kernel, which, grid, slots)
        return call(kernel, shape(slots, BLOCK * BLOCK), [VM] * 6 + [HB], VM, scratch, name)(
            idents, *own[:2], *parts, stay(earlier)
        )

    first_out = final_of(0, first, first_parts, flat_data(density), "first_final")
    second_out = final_of(1, second, second_parts, first_out, "second_final")
    return first_out.reshape(density.shape), second_out.reshape(density.shape)


def solution(mesh):
    data = P(("groups", "row"), "col", None, None, None)
    pattern = P(("groups", "row"), "col", None, None)
    return jax.shard_map(
        shards,
        mesh=mesh,
        in_specs=(data, pattern, data, pattern, pattern, pattern, pattern, pattern),
        out_specs=(data, data),
        check_vma=False,
    )
```

```python
import functools

import jax
import jax.numpy as jnp
from jax import lax
from jax.experimental import pallas as pl
from jax.experimental.pallas import tpu as pltpu
from jax.sharding import PartitionSpec as P

BLOCK = 64
WIDE = 2 * BLOCK
HALF = BLOCK // 2
DEPTH = 3 * BLOCK
ASK_ROWS = BLOCK + HALF
PADS = (16, 0, 0, 8, 8, 16, 0, 8)
F32 = jnp.float32
BF16 = jnp.bfloat16
VMEM_LIMIT = 16 * 1024 * 1024


def on_left(rows):
    return lax.broadcasted_iota(jnp.int32, (rows, WIDE), 1) < BLOCK


def swap(tile):
    return pltpu.roll(tile, BLOCK, 1)


def place_of(ident, grid):
    rows, cols = grid
    source = jnp.maximum(ident, 0)
    owner_row = lax.div(source, jnp.int32(cols))
    owner_col = lax.rem(source, jnp.int32(cols))
    down = lax.rem(owner_row - lax.axis_index("row") + 1 + rows, jnp.int32(rows))
    across = lax.rem(owner_col - lax.axis_index("col") + 1 + cols, jnp.int32(cols))
    return jnp.where(ident < 0, 9, down * 3 + across)


def note_slots(which, pattern, table, grid, slots):
    for place in range(10):
        table[which, place] = slots
    for slot in range(slots):
        table[which, place_of(pattern[0, slot], grid)] = slot


def ident_at(place, grid):
    rows, cols = grid
    row = lax.rem(lax.axis_index("row") + place // 3 - 1 + rows, jnp.int32(rows))
    col = lax.rem(lax.axis_index("col") + place % 3 - 1 + cols, jnp.int32(cols))
    return (row * cols + col).astype(F32)


def pair_at(low, high, grid):
    return jnp.where(on_left(1), ident_at(low, grid), ident_at(high, grid))


def is_live(idents, wanted):
    return jnp.max(jnp.where(idents == wanted, 1.0, 0.0), axis=0, keepdims=True) > 0


def tile_at(e):
    return slice(e * BLOCK, (e + 1) * BLOCK)


def fetch(sources, targets, sems):
    copies = [pltpu.make_async_copy(s, t, sems.at[i]) for i, (s, t) in enumerate(zip(sources, targets))]
    for copy in copies:
        copy.start()
    return copies


def fill_rest(message):
    if message.shape[0] > DEPTH:
        message[DEPTH:, :] = jnp.zeros((message.shape[0] - DEPTH, WIDE), F32)


def spread(which, slots, data, to_left, to_right, rows, table):
    first_half = on_left(HALF)
    rows[slots * HALF : (slots + 1) * HALF, :] = jnp.zeros((HALF, WIDE), F32)
    for step in range(HALF):
        rows[pl.ds(step, slots, stride=HALF), :] = data[:, step * WIDE : (step + 1) * WIDE]

    def block(place):
        own = rows[pl.ds(pl.multiple_of(table[which, place] * HALF, HALF), HALF), :]
        return own, swap(own)

    def tile(low, high):
        return (jnp.where(first_half, low[0], high[1]), jnp.where(first_half, low[1], high[0]))

    for e in range(3):
        a, b, c = block(3 * e), block(3 * e + 1), block(3 * e + 2)
        left, right = tile(a, b), tile(b, c)
        for part in range(2):
            to_left[pl.ds(e * BLOCK + part, HALF, stride=2), :] = left[part]
            to_right[pl.ds(e * BLOCK + part, HALF, stride=2), :] = right[part]
    fill_rest(to_left)
    fill_rest(to_right)


def spread_kernel(grid, slots, *refs):
    sources, (first_left, first_right, second_left, second_right, idents) = refs[:8], refs[8:13]
    patterns, datas, later, (rows, table, sems) = refs[13:15], refs[15:17], refs[17:21], refs[21:]
    copies = fetch(sources, (*patterns, *datas, *later), sems)
    for which, pattern in enumerate(patterns):
        copies[which].wait()
        note_slots(which, pattern, table, grid, slots)
    for which, pattern in enumerate(later):
        copies[4 + which].wait()
        for slot in range(slots):
            idents[which, slot : slot + 1, :] = jnp.full((1, WIDE), pattern[0, slot].astype(F32), F32)
    for which, pair in enumerate(((first_left, first_right), (second_left, second_right))):
        copies[2 + which].wait()
        spread(which, slots, datas[which], *pair, rows.at[which], table)


def ask_kernel(slots, first_left, first_right, second_left, second_right, idents, ask_last, ask_next):
    for which, (left, right) in enumerate(((first_left, first_right), (second_left, second_right))):
        at = which * ASK_ROWS
        for ask, e in ((ask_last, 0), (ask_next, 2)):
            ask[at : at + BLOCK, :] = left[tile_at(e)]
            ask[at + BLOCK : at + ASK_ROWS, :] = fold(right[tile_at(e)])
            masks = 2 * ASK_ROWS + slots * which
            ask[masks : masks + slots, :] = idents[which]


def fold(right):
    return jnp.where(on_left(HALF), swap(right[:HALF]), right[HALF:])


def split(tile):
    high = tile.astype(BF16)
    return high, (tile - high.astype(F32)).astype(BF16)


def put_depth(factor, rows, tile):
    high, low = split(tile)
    for part, value in enumerate((high, low, high)):
        factor[rows, part * WIDE : (part + 1) * WIDE] = value


def fill_left_factor(at, left, right, factor):
    rows = tile_at(at)
    put_depth(factor.at[0], rows, left)
    put_depth(factor.at[1], rows, right)


def unfold(left, folded):
    first = on_left(HALF)
    other = jnp.concatenate([jnp.where(first, folded, swap(folded)), jnp.where(first, swap(folded), folded)], axis=0)
    return jnp.where(on_left(BLOCK), swap(left), other)


def fill_right_factor(own_left, own_right, from_left, from_right, factor):
    first = on_left(BLOCK)
    for e in range(3):
        at = pl.ds(e * WIDE, WIDE)
        near = jnp.where(first, 0.0, own_right[tile_at(e)])
        for side, pair in enumerate(((from_left[tile_at(e)], own_left[tile_at(e)]), (near, from_right[tile_at(e)]))):
            for k, tile in enumerate(pair):
                high, low = split(tile)
                for part, value in enumerate((high, high, low)):
                    factor[side, tile_at(2 * part + k), at] = value


def product(factor, by):
    return [
        lax.dot_general(factor[side], by[side], (((1,), (0,)), ((), ())), preferred_element_type=F32)
        for side in range(2)
    ]


def tiles_of(total, at, low, count):
    first = on_left(BLOCK)
    left, right = [], []
    for e in range(low, low + count):
        a, b = (side[tile_at(at), e * WIDE : (e + 1) * WIDE] for side in total)
        left.append(a + jnp.where(first, 0.0, swap(b)))
        right.append(b)
    return left, right


def put_all(total, to_last, to_next, sums):
    for at, low, share in ((0, 0, to_last), (1, 1, to_next)):
        left, right = tiles_of(total, at, low, 2)
        share[:BLOCK, :] = left[0]
        share[BLOCK:WIDE, :] = left[1]
        share[WIDE:DEPTH, :] = jnp.where(on_left(BLOCK), swap(right[0]), right[1])
    left, right = tiles_of(total, 2, 0, 3)
    for e in range(3):
        sums[e] = left[e]
        sums[3 + e] = right[e]
    for share, e in ((to_last, 0), (to_next, 2)):
        if share.shape[0] > DEPTH:
            share[DEPTH : DEPTH + BLOCK, :] = left[e]
            share[DEPTH + BLOCK :, :] = fold(right[e])


def fill_own(left, right, factor):
    fill_left_factor(2, left[tile_at(1)], right[tile_at(1)], factor)


def fill_asked(which, grid, slots, asks, got, sent, factor):
    for at in range(2):
        if got is None:
            row = which * ASK_ROWS
            left, folded = asks[at][row : row + BLOCK], asks[at][row + BLOCK : row + ASK_ROWS]
        else:
            pack = sent[at][WIDE:DEPTH]
            if at == 0:
                left, folded = sent[at][BLOCK:WIDE], fold(pack)
            else:
                left, folded = sent[at][:BLOCK], jnp.where(on_left(HALF), pack[:HALF], swap(pack[HALF:]))
            row = 2 * ASK_ROWS + slots * which
            idents = asks[at][row : row + slots]
            left = jnp.where(is_live(idents, pair_at(3, 4, grid)), left + got[at][DEPTH : DEPTH + BLOCK], 0.0)
            folded = jnp.where(is_live(idents, ident_at(5, grid)), folded + got[at][DEPTH + BLOCK :], 0.0)
        fill_left_factor(at, left, unfold(left, folded), factor)


def first_share_kernel(grid, slots, earlier, *refs):
    tiles, asks, refs = refs[:4], refs[4:6], refs[6:]
    got, sent = (refs[:2], refs[2:4]) if earlier else (None, None)
    to_last, to_next, sums, by, factor = refs[4 if earlier else 0 :]
    fill_right_factor(*tiles, by)
    fill_asked(0, grid, slots, asks, got, sent, factor)
    fill_own(tiles[0], tiles[1], factor)
    put_all(product(factor, by), to_last, to_next, sums)


def second_share_kernel(grid, slots, earlier, *refs):
    tiles, asks, refs = refs[:4], refs[4:6], refs[6:]
    got, sent = (refs[:2], refs[2:4]) if earlier else (None, None)
    first_by, first_factor, to_last, to_next, sums, by, factor = refs[4 if earlier else 0 :]
    fill_right_factor(*tiles, by)
    fill_asked(1, grid, slots, asks, got, sent, factor)
    fill_own(tiles[0], tiles[1], factor)
    both = [a + b for a, b in zip(product(factor, first_by), product(first_factor, by))]
    put_all(both, to_last, to_next, sums)


def total(sums, from_last, from_next):
    left = [sums[e] for e in range(3)]
    right = [sums[3 + e] for e in range(3)]
    for share, low in ((from_last, 0), (from_next, 1)):
        pack = share[WIDE:DEPTH]
        left[low] += share[:BLOCK]
        left[low + 1] += share[BLOCK:WIDE]
        right[low] += swap(pack)
        right[low + 1] += pack
    return left, right


def next_kernel(which, grid, idents, sums, from_last, from_next, to_left, to_right):
    first = on_left(BLOCK)
    left, right = total(sums, from_last, from_next)
    for e in range(3):
        keep_left = is_live(idents[which], pair_at(3 * e, 3 * e + 1, grid))
        keep_right = is_live(idents[which], pair_at(3 * e + 1, 3 * e + 2, grid))
        to_left[tile_at(e), :] = jnp.where(keep_left, left[e], 0.0)
        to_right[tile_at(e), :] = jnp.where(keep_right, jnp.where(first, swap(left[e]), right[e]), 0.0)
    fill_rest(to_left)
    fill_rest(to_right)


def final_kernel(which, grid, slots, idents, own_left, own_right, sums, from_last, from_next, _, out, dense, packed):
    first_half = on_left(HALF)
    even, odd = pl.ds(0, HALF, stride=2), pl.ds(1, HALF, stride=2)
    left, right = total(sums, from_last, from_next)
    for e in range(3):
        dense[e] = 2.0 * own_left[tile_at(e)] - left[e]
        dense[3 + e] = 2.0 * own_right[tile_at(e)] - right[e]
    for e in range(3):
        a, b = dense[e, even, :], dense[e, odd, :]
        packed[3 * e] = jnp.where(first_half, a, swap(b))
        packed[3 * e + 1] = jnp.where(first_half, swap(a), b)
        a, b = dense[3 + e, even, :], dense[3 + e, odd, :]
        packed[3 * e + 2] = jnp.where(first_half, swap(a), b)
    slot_holds = [idents[2 + which] == ident_at(place, grid) for place in range(9)]
    for step in range(HALF):
        line = jnp.zeros((slots, WIDE), F32)
        for place in range(9):
            line = jnp.where(slot_holds[place], packed[place, step : step + 1, :], line)
        out[:, step * WIDE : (step + 1) * WIDE] = line


def shift(block, axis, by):
    count = lax.axis_size(axis)
    return lax.ppermute(block, axis, [(i, (i + by) % count) for i in range(count)])


VM = pl.BlockSpec(memory_space=pltpu.VMEM)
HB = pl.BlockSpec(memory_space=pltpu.HBM)
PARAMS = pltpu.CompilerParams(vmem_limit_bytes=VMEM_LIMIT)


def stay(operand):
    return pltpu.with_memory_space_constraint(operand, pltpu.HBM)


def shape(*sizes):
    return jax.ShapeDtypeStruct(sizes, F32)


def call(kernel, out_shape, in_specs, out_specs, scratch, name, flops=0):
    return pl.pallas_call(
        kernel,
        out_shape=out_shape,
        in_specs=in_specs,
        out_specs=out_specs,
        scratch_shapes=scratch,
        compiler_params=PARAMS,
        cost_estimate=pl.CostEstimate(flops=flops, bytes_accessed=10**6, transcendentals=0),
        name=name,
    )


def tiles_shape(rest):
    return shape(DEPTH + rest, WIDE)


SHARE = shape(DEPTH, WIDE)
LONG_SHARE = shape(DEPTH + ASK_ROWS, WIDE)
SUMS = shape(6, BLOCK, WIDE)
BY_SHAPE = (2, 3 * WIDE, 3 * WIDE)
FACTOR_SHAPE = (2, 3 * BLOCK, 3 * WIDE)


def call_all(kernel, outputs, operands, scratch, name):
    return call(kernel, outputs, [VM] * len(operands), [VM] * len(outputs), scratch, name)(*operands)


def along_col(to_left, to_right):
    return to_left, to_right, shift(to_right, "col", 1), shift(to_left, "col", -1)


def along_row(to_last, to_next):
    return shift(to_next, "row", 1), shift(to_last, "row", -1)


def shards(
    density,
    density_pattern,
    response,
    response_pattern,
    density_next_pattern,
    response_next_pattern,
    density_out_pattern,
    response_out_pattern,
):
    slots = density.shape[3]
    grid = (lax.axis_size("row"), lax.axis_size("col"))
    pattern_scratch = pltpu.SMEM((1, slots), jnp.int32)
    table = pltpu.SMEM((2, 16), jnp.int32)

    def flat(pattern):
        return stay(pattern.reshape(1, slots))

    def flat_data(data):
        return stay(data.reshape(slots, BLOCK * BLOCK))

    *tiles, idents = call(
        functools.partial(spread_kernel, grid, slots),
        [tiles_shape(r) for r in PADS[:4]] + [shape(4, slots, WIDE)],
        [HB] * 8,
        [VM] * 5,
        [pattern_scratch] * 2
        + [pltpu.VMEM((slots, BLOCK * BLOCK), F32)] * 2
        + [pattern_scratch] * 4
        + [pltpu.VMEM((2, (slots + 1) * HALF, WIDE), F32), table, pltpu.SemaphoreType.DMA((8,))],
        "spread",
    )(
        flat(density_pattern),
        flat(response_pattern),
        flat_data(density),
        flat_data(response),
        flat(density_next_pattern),
        flat(response_next_pattern),
        flat(density_out_pattern),
        flat(response_out_pattern),
    )

    def share(first, second, asks, shape_of_share, earlier):
        outputs = [shape_of_share] * 2 + [SUMS]
        factors = [jax.ShapeDtypeStruct(BY_SHAPE, BF16), jax.ShapeDtypeStruct(FACTOR_SHAPE, BF16)]
        scratch = [pltpu.VMEM(BY_SHAPE, BF16), pltpu.VMEM(FACTOR_SHAPE, BF16)]
        *first_sent, first_sums, first_by, first_factor = call_all(
            functools.partial(first_share_kernel, grid, slots, bool(earlier)),
            outputs + factors,
            (*first, *asks, *(earlier[0] if earlier else ())),
            [],
            "first_share",
        )
        first_got = along_row(*first_sent)
        *second_sent, second_sums = call_all(
            functools.partial(second_share_kernel, grid, slots, bool(earlier)),
            outputs,
            (*second, *asks, *(earlier[1] if earlier else ()), first_by, first_factor),
            scratch,
            "second_share",
        )
        second_got = along_row(*second_sent)
        return (first_sums, *first_got), (second_sums, *second_got), first_sent, second_sent

    first = along_col(*tiles[:2])
    asks = along_row(
        *call_all(
            functools.partial(ask_kernel, slots),
            [shape(2 * (ASK_ROWS + slots), WIDE)] * 2,
            (*tiles, idents),
            [],
            "ask",
        )
    )
    second = along_col(*tiles[2:])
    first_parts, second_parts, first_sent, second_sent = share(first, second, asks, LONG_SHARE, ())
    earlier = ((*first_parts[1:], *first_sent), (*second_parts[1:], *second_sent))
    next_tiles = [
        call_all(
            functools.partial(next_kernel, which, grid),
            [tiles_shape(r) for r in PADS[4 + 2 * which : 6 + 2 * which]],
            (idents, *parts),
            [],
            name,
        )
        for which, parts, name in ((0, first_parts, "first_next"), (1, second_parts, "second_next"))
    ]
    first, second = along_col(*next_tiles[0]), along_col(*next_tiles[1])
    first_parts, second_parts, _, _ = share(first, second, asks, SHARE, earlier)

    def final_of(which, own, parts, earlier, name):
        scratch = [pltpu.VMEM((6, BLOCK, WIDE), F32), pltpu.VMEM((9, HALF, WIDE), F32)]
        kernel = functools.partial(final_kernel, which, grid, slots)
        return call(kernel, shape(slots, BLOCK * BLOCK), [VM] * 6 + [HB], VM, scratch, name)(
            idents, *own[:2], *parts, stay(earlier)
        )

    first_out = final_of(0, first, first_parts, flat_data(density), "first_final")
    second_out = final_of(1, second, second_parts, first_out, "second_final")
    return first_out.reshape(density.shape), second_out.reshape(density.shape)


def solution(mesh):
    data = P(("groups", "row"), "col", None, None, None)
    pattern = P(("groups", "row"), "col", None, None)
    return jax.shard_map(
        shards,
        mesh=mesh,
        in_specs=(data, pattern, data, pattern, pattern, pattern, pattern, pattern),
        out_specs=(data, data),
        check_vma=False,
    )
```

```python
import functools

import jax
import jax.numpy as jnp
from jax import lax
from jax.experimental import pallas as pl
from jax.experimental.pallas import tpu as pltpu
from jax.sharding import PartitionSpec as P

BLOCK = 64
WIDE = 2 * BLOCK
HALF = BLOCK // 2
DEPTH = 3 * BLOCK
ASK_ROWS = BLOCK + HALF
PADS = (16, 0, 0, 8, 8, 16, 0, 8)
NEAR_PAD = 8
F32 = jnp.float32
BF16 = jnp.bfloat16
VMEM_LIMIT = 16 * 1024 * 1024


def on_left(rows):
    return lax.broadcasted_iota(jnp.int32, (rows, WIDE), 1) < BLOCK


def swap(tile):
    return pltpu.roll(tile, BLOCK, 1)


def place_of(ident, grid):
    rows, cols = grid
    source = jnp.maximum(ident, 0)
    owner_row = lax.div(source, jnp.int32(cols))
    owner_col = lax.rem(source, jnp.int32(cols))
    down = lax.rem(owner_row - lax.axis_index("row") + 1 + rows, jnp.int32(rows))
    across = lax.rem(owner_col - lax.axis_index("col") + 1 + cols, jnp.int32(cols))
    return jnp.where(ident < 0, 9, down * 3 + across)


def note_slots(which, pattern, table, grid, slots):
    for place in range(10):
        table[which, place] = slots
    for slot in range(slots):
        table[which, place_of(pattern[0, slot], grid)] = slot


def ident_at(place, grid):
    rows, cols = grid
    row = lax.rem(lax.axis_index("row") + place // 3 - 1 + rows, jnp.int32(rows))
    col = lax.rem(lax.axis_index("col") + place % 3 - 1 + cols, jnp.int32(cols))
    return (row * cols + col).astype(F32)


def pair_at(low, high, grid):
    return jnp.where(on_left(1), ident_at(low, grid), ident_at(high, grid))


def is_live(idents, wanted):
    return jnp.max(jnp.where(idents == wanted, 1.0, 0.0), axis=0, keepdims=True) > 0


def tile_at(e):
    return slice(e * BLOCK, (e + 1) * BLOCK)


def fetch(sources, targets, sems):
    copies = [pltpu.make_async_copy(s, t, sems.at[i]) for i, (s, t) in enumerate(zip(sources, targets))]
    for copy in copies:
        copy.start()
    return copies


def fill_rest(message):
    if message.shape[0] > DEPTH:
        message[DEPTH:, :] = jnp.zeros((message.shape[0] - DEPTH, WIDE), F32)


def spread(which, slots, data, to_left, to_right, rows, table):
    first_half = on_left(HALF)
    rows[slots * HALF : (slots + 1) * HALF, :] = jnp.zeros((HALF, WIDE), F32)
    for step in range(HALF):
        rows[pl.ds(step, slots, stride=HALF), :] = data[:, step * WIDE : (step + 1) * WIDE]

    def block(place):
        own = rows[pl.ds(pl.multiple_of(table[which, place] * HALF, HALF), HALF), :]
        return own, swap(own)

    def tile(low, high):
        return (jnp.where(first_half, low[0], high[1]), jnp.where(first_half, low[1], high[0]))

    for e in range(3):
        a, b, c = block(3 * e), block(3 * e + 1), block(3 * e + 2)
        left, right = tile(a, b), tile(b, c)
        for part in range(2):
            to_left[pl.ds(e * BLOCK + part, HALF, stride=2), :] = left[part]
            to_right[pl.ds(e * BLOCK + part, HALF, stride=2), :] = right[part]
    fill_rest(to_left)
    fill_rest(to_right)


def spread_kernel(grid, slots, *refs):
    sources, (first_left, first_right, second_left, second_right, idents) = refs[:8], refs[8:13]
    patterns, datas, later, (rows, table, sems) = refs[13:15], refs[15:17], refs[17:21], refs[21:]
    copies = fetch(sources, (*patterns, *datas, *later), sems)
    for which, pattern in enumerate(patterns):
        copies[which].wait()
        note_slots(which, pattern, table, grid, slots)
    for which, pattern in enumerate(later):
        copies[4 + which].wait()
        for slot in range(slots):
            idents[which, slot : slot + 1, :] = jnp.full((1, WIDE), pattern[0, slot].astype(F32), F32)
    for which, pair in enumerate(((first_left, first_right), (second_left, second_right))):
        copies[2 + which].wait()
        spread(which, slots, datas[which], *pair, rows.at[which], table)


def is_even():
    return lax.rem(lax.axis_index("row"), 2) == 0


def ask_kernel(slots, first_left, first_right, second_left, second_right, idents, far, near):
    even = is_even()
    for which, (left, right) in enumerate(((first_left, first_right), (second_left, second_right))):
        at = which * ASK_ROWS
        last, following = left[tile_at(0)], left[tile_at(2)]
        near[at : at + BLOCK, :] = jnp.where(even, following, last)
        far[at : at + BLOCK, :] = jnp.where(even, last, following)
        last, following = fold(right[tile_at(0)]), fold(right[tile_at(2)])
        near[at + BLOCK : at + ASK_ROWS, :] = jnp.where(even, following, last)
        far[at + BLOCK : at + ASK_ROWS, :] = jnp.where(even, last, following)
        masks = 2 * ASK_ROWS + slots * which
        near[masks : masks + slots, :] = idents[which]
        far[masks : masks + slots, :] = idents[which]
    rest = 2 * (ASK_ROWS + slots)
    if near.shape[0] > rest:
        near[rest:, :] = jnp.zeros((near.shape[0] - rest, WIDE), F32)


def fold(right):
    return jnp.where(on_left(HALF), swap(right[:HALF]), right[HALF:])


def split(tile):
    high = tile.astype(BF16)
    return high, (tile - high.astype(F32)).astype(BF16)


def put_depth(factor, rows, tile):
    high, low = split(tile)
    for part, value in enumerate((high, low, high)):
        factor[rows, part * WIDE : (part + 1) * WIDE] = value


def fill_left_factor(at, left, right, factor):
    rows = tile_at(at)
    put_depth(factor.at[0], rows, left)
    put_depth(factor.at[1], rows, right)


def unfold(left, folded):
    first = on_left(HALF)
    other = jnp.concatenate([jnp.where(first, folded, swap(folded)), jnp.where(first, swap(folded), folded)], axis=0)
    return jnp.where(on_left(BLOCK), swap(left), other)


def fill_right_factor(own_left, own_right, from_left, from_right, factor):
    first = on_left(BLOCK)
    for e in range(3):
        at = pl.ds(e * WIDE, WIDE)
        near = jnp.where(first, 0.0, own_right[tile_at(e)])
        for side, pair in enumerate(((from_left[tile_at(e)], own_left[tile_at(e)]), (near, from_right[tile_at(e)]))):
            for k, tile in enumerate(pair):
                high, low = split(tile)
                for part, value in enumerate((high, high, low)):
                    factor[side, tile_at(2 * part + k), at] = value


def product(factor, by):
    return [
        lax.dot_general(factor[side], by[side], (((1,), (0,)), ((), ())), preferred_element_type=F32)
        for side in range(2)
    ]


def tiles_of(total, at, low, count):
    first = on_left(BLOCK)
    left, right = [], []
    for e in range(low, low + count):
        a, b = (side[tile_at(at), e * WIDE : (e + 1) * WIDE] for side in total)
        left.append(a + jnp.where(first, 0.0, swap(b)))
        right.append(b)
    return left, right


def put_all(total, to_last, to_next, sums):
    for at, low, share in ((0, 0, to_last), (1, 1, to_next)):
        left, right = tiles_of(total, at, low, 2)
        share[:BLOCK, :] = left[0]
        share[BLOCK:WIDE, :] = left[1]
        share[WIDE:DEPTH, :] = jnp.where(on_left(BLOCK), swap(right[0]), right[1])
    left, right = tiles_of(total, 2, 0, 3)
    for e in range(3):
        sums[e] = left[e]
        sums[3 + e] = right[e]
    for share, e in ((to_last, 0), (to_next, 2)):
        if share.shape[0] > DEPTH:
            share[DEPTH : DEPTH + BLOCK, :] = left[e]
            share[DEPTH + BLOCK :, :] = fold(right[e])


def fill_own(left, right, factor):
    fill_left_factor(2, left[tile_at(1)], right[tile_at(1)], factor)


def fill_asked(which, grid, slots, asks, got, sent, factor):
    far, near = asks
    even = is_even()
    for at in range(2):
        from_far = even if at == 0 else jnp.logical_not(even)

        def asked(start, count):
            return jnp.where(from_far, far[start : start + count], near[start : start + count])

        if got is None:
            row = which * ASK_ROWS
            left, folded = asked(row, BLOCK), asked(row + BLOCK, HALF)
        else:
            pack = sent[at][WIDE:DEPTH]
            if at == 0:
                left, folded = sent[at][BLOCK:WIDE], fold(pack)
            else:
                left, folded = sent[at][:BLOCK], jnp.where(on_left(HALF), pack[:HALF], swap(pack[HALF:]))
            idents = asked(2 * ASK_ROWS + slots * which, slots)
            left = jnp.where(is_live(idents, pair_at(3, 4, grid)), left + got[at][DEPTH : DEPTH + BLOCK], 0.0)
            folded = jnp.where(is_live(idents, ident_at(5, grid)), folded + got[at][DEPTH + BLOCK :], 0.0)
        fill_left_factor(at, left, unfold(left, folded), factor)


def first_share_kernel(grid, slots, earlier, *refs):
    tiles, asks, refs = refs[:4], refs[4:6], refs[6:]
    got, sent = (refs[:2], refs[2:4]) if earlier else (None, None)
    to_last, to_next, sums, by, factor = refs[4 if earlier else 0 :]
    fill_right_factor(*tiles, by)
    fill_asked(0, grid, slots, asks, got, sent, factor)
    fill_own(tiles[0], tiles[1], factor)
    put_all(product(factor, by), to_last, to_next, sums)


def second_share_kernel(grid, slots, earlier, *refs):
    tiles, asks, refs = refs[:4], refs[4:6], refs[6:]
    got, sent = (refs[:2], refs[2:4]) if earlier else (None, None)
    first_by, first_factor, to_last, to_next, sums, by, factor = refs[4 if earlier else 0 :]
    fill_right_factor(*tiles, by)
    fill_asked(1, grid, slots, asks, got, sent, factor)
    fill_own(tiles[0], tiles[1], factor)
    both = [a + b for a, b in zip(product(factor, first_by), product(first_factor, by))]
    put_all(both, to_last, to_next, sums)


def total(sums, from_last, from_next):
    left = [sums[e] for e in range(3)]
    right = [sums[3 + e] for e in range(3)]
    for share, low in ((from_last, 0), (from_next, 1)):
        pack = share[WIDE:DEPTH]
        left[low] += share[:BLOCK]
        left[low + 1] += share[BLOCK:WIDE]
        right[low] += swap(pack)
        right[low + 1] += pack
    return left, right


def next_kernel(which, grid, idents, sums, from_last, from_next, to_left, to_right):
    first = on_left(BLOCK)
    left, right = total(sums, from_last, from_next)
    for e in range(3):
        keep_left = is_live(idents[which], pair_at(3 * e, 3 * e + 1, grid))
        keep_right = is_live(idents[which], pair_at(3 * e + 1, 3 * e + 2, grid))
        to_left[tile_at(e), :] = jnp.where(keep_left, left[e], 0.0)
        to_right[tile_at(e), :] = jnp.where(keep_right, jnp.where(first, swap(left[e]), right[e]), 0.0)
    fill_rest(to_left)
    fill_rest(to_right)


def final_kernel(which, grid, slots, idents, own_left, own_right, sums, from_last, from_next, _, out, dense, packed):
    first_half = on_left(HALF)
    even, odd = pl.ds(0, HALF, stride=2), pl.ds(1, HALF, stride=2)
    left, right = total(sums, from_last, from_next)
    for e in range(3):
        dense[e] = 2.0 * own_left[tile_at(e)] - left[e]
        dense[3 + e] = 2.0 * own_right[tile_at(e)] - right[e]
    for e in range(3):
        a, b = dense[e, even, :], dense[e, odd, :]
        packed[3 * e] = jnp.where(first_half, a, swap(b))
        packed[3 * e + 1] = jnp.where(first_half, swap(a), b)
        a, b = dense[3 + e, even, :], dense[3 + e, odd, :]
        packed[3 * e + 2] = jnp.where(first_half, swap(a), b)
    slot_holds = [idents[2 + which] == ident_at(place, grid) for place in range(9)]
    for step in range(HALF):
        line = jnp.zeros((slots, WIDE), F32)
        for place in range(9):
            line = jnp.where(slot_holds[place], packed[place, step : step + 1, :], line)
        out[:, step * WIDE : (step + 1) * WIDE] = line


def shift(block, axis, by):
    count = lax.axis_size(axis)
    return lax.ppermute(block, axis, [(i, (i + by) % count) for i in range(count)])


VM = pl.BlockSpec(memory_space=pltpu.VMEM)
HB = pl.BlockSpec(memory_space=pltpu.HBM)
PARAMS = pltpu.CompilerParams(vmem_limit_bytes=VMEM_LIMIT)


def stay(operand):
    return pltpu.with_memory_space_constraint(operand, pltpu.HBM)


def shape(*sizes):
    return jax.ShapeDtypeStruct(sizes, F32)


def call(kernel, out_shape, in_specs, out_specs, scratch, name, flops=0):
    return pl.pallas_call(
        kernel,
        out_shape=out_shape,
        in_specs=in_specs,
        out_specs=out_specs,
        scratch_shapes=scratch,
        compiler_params=PARAMS,
        cost_estimate=pl.CostEstimate(flops=flops, bytes_accessed=10**6, transcendentals=0),
        name=name,
    )


def tiles_shape(rest):
    return shape(DEPTH + rest, WIDE)


SHARE = shape(DEPTH, WIDE)
LONG_SHARE = shape(DEPTH + ASK_ROWS, WIDE)
SUMS = shape(6, BLOCK, WIDE)
BY_SHAPE = (2, 3 * WIDE, 3 * WIDE)
FACTOR_SHAPE = (2, 3 * BLOCK, 3 * WIDE)


def call_all(kernel, outputs, operands, scratch, name):
    return call(kernel, outputs, [VM] * len(operands), [VM] * len(outputs), scratch, name)(*operands)


def along_col(to_left, to_right):
    return to_left, to_right, shift(to_right, "col", 1), shift(to_left, "col", -1)


def along_row(to_last, to_next):
    return shift(to_next, "row", 1), shift(to_last, "row", -1)


def in_pairs(far, near):
    rows = lax.axis_size("row")
    far = lax.ppermute(far, "row", [(i, (((i + 1) ^ 1) - 1) % rows) for i in range(rows)])
    return far, lax.ppermute(near, "row", [(i, i ^ 1) for i in range(rows)])


def shards(
    density,
    density_pattern,
    response,
    response_pattern,
    density_next_pattern,
    response_next_pattern,
    density_out_pattern,
    response_out_pattern,
):
    slots = density.shape[3]
    grid = (lax.axis_size("row"), lax.axis_size("col"))
    pattern_scratch = pltpu.SMEM((1, slots), jnp.int32)
    table = pltpu.SMEM((2, 16), jnp.int32)

    def flat(pattern):
        return stay(pattern.reshape(1, slots))

    def flat_data(data):
        return stay(data.reshape(slots, BLOCK * BLOCK))

    *tiles, idents = call(
        functools.partial(spread_kernel, grid, slots),
        [tiles_shape(r) for r in PADS[:4]] + [shape(4, slots, WIDE)],
        [HB] * 8,
        [VM] * 5,
        [pattern_scratch] * 2
        + [pltpu.VMEM((slots, BLOCK * BLOCK), F32)] * 2
        + [pattern_scratch] * 4
        + [pltpu.VMEM((2, (slots + 1) * HALF, WIDE), F32), table, pltpu.SemaphoreType.DMA((8,))],
        "spread",
    )(
        flat(density_pattern),
        flat(response_pattern),
        flat_data(density),
        flat_data(response),
        flat(density_next_pattern),
        flat(response_next_pattern),
        flat(density_out_pattern),
        flat(response_out_pattern),
    )

    def share(first, second, asks, shape_of_share, earlier):
        outputs = [shape_of_share] * 2 + [SUMS]
        factors = [jax.ShapeDtypeStruct(BY_SHAPE, BF16), jax.ShapeDtypeStruct(FACTOR_SHAPE, BF16)]
        scratch = [pltpu.VMEM(BY_SHAPE, BF16), pltpu.VMEM(FACTOR_SHAPE, BF16)]
        *first_sent, first_sums, first_by, first_factor = call_all(
            functools.partial(first_share_kernel, grid, slots, bool(earlier)),
            outputs + factors,
            (*first, *asks, *(earlier[0] if earlier else ())),
            [],
            "first_share",
        )
        first_got = along_row(*first_sent)
        *second_sent, second_sums = call_all(
            functools.partial(second_share_kernel, grid, slots, bool(earlier)),
            outputs,
            (*second, *asks, *(earlier[1] if earlier else ()), first_by, first_factor),
            scratch,
            "second_share",
        )
        second_got = along_row(*second_sent)
        return (first_sums, *first_got), (second_sums, *second_got), first_sent, second_sent

    first = along_col(*tiles[:2])
    asks = in_pairs(
        *call_all(
            functools.partial(ask_kernel, slots),
            [shape(2 * (ASK_ROWS + slots) + rest, WIDE) for rest in (0, NEAR_PAD)],
            (*tiles, idents),
            [],
            "ask",
        )
    )
    second = along_col(*tiles[2:])
    first_parts, second_parts, first_sent, second_sent = share(first, second, asks, LONG_SHARE, ())
    earlier = ((*first_parts[1:], *first_sent), (*second_parts[1:], *second_sent))
    next_tiles = [
        call_all(
            functools.partial(next_kernel, which, grid),
            [tiles_shape(r) for r in PADS[4 + 2 * which : 6 + 2 * which]],
            (idents, *parts),
            [],
            name,
        )
        for which, parts, name in ((0, first_parts, "first_next"), (1, second_parts, "second_next"))
    ]
    first, second = along_col(*next_tiles[0]), along_col(*next_tiles[1])
    first_parts, second_parts, _, _ = share(first, second, asks, SHARE, earlier)

    def final_of(which, own, parts, earlier, name):
        scratch = [pltpu.VMEM((6, BLOCK, WIDE), F32), pltpu.VMEM((9, HALF, WIDE), F32)]
        kernel = functools.partial(final_kernel, which, grid, slots)
        return call(kernel, shape(slots, BLOCK * BLOCK), [VM] * 6 + [HB], VM, scratch, name)(
            idents, *own[:2], *parts, stay(earlier)
        )

    first_out = final_of(0, first, first_parts, flat_data(density), "first_final")
    second_out = final_of(1, second, second_parts, first_out, "second_final")
    return first_out.reshape(density.shape), second_out.reshape(density.shape)


def solution(mesh):
    data = P(("groups", "row"), "col", None, None, None)
    pattern = P(("groups", "row"), "col", None, None)
    return jax.shard_map(
        shards,
        mesh=mesh,
        in_specs=(data, pattern, data, pattern, pattern, pattern, pattern, pattern),
        out_specs=(data, data),
        check_vma=False,
    )
```

```python
import functools

import jax
import jax.numpy as jnp
from jax import lax
from jax.experimental import pallas as pl
from jax.experimental.pallas import tpu as pltpu
from jax.sharding import PartitionSpec as P

BLOCK = 64
WIDE = 2 * BLOCK
HALF = BLOCK // 2
DEPTH = 3 * BLOCK
ASK_ROWS = BLOCK + HALF
PADS = (16, 0, 0, 8, 8, 16, 0, 8)
NEAR_PAD = 8
SHARE_PADS = (8, 8), (0, 8)
F32 = jnp.float32
BF16 = jnp.bfloat16
VMEM_LIMIT = 16 * 1024 * 1024


def on_left(rows):
    return lax.broadcasted_iota(jnp.int32, (rows, WIDE), 1) < BLOCK


def swap(tile):
    return pltpu.roll(tile, BLOCK, 1)


def place_of(ident, grid):
    rows, cols = grid
    source = jnp.maximum(ident, 0)
    owner_row = lax.div(source, jnp.int32(cols))
    owner_col = lax.rem(source, jnp.int32(cols))
    down = lax.rem(owner_row - lax.axis_index("row") + 1 + rows, jnp.int32(rows))
    across = lax.rem(owner_col - lax.axis_index("col") + 1 + cols, jnp.int32(cols))
    return jnp.where(ident < 0, 9, down * 3 + across)


def note_slots(which, pattern, table, grid, slots):
    for place in range(10):
        table[which, place] = slots
    for slot in range(slots):
        table[which, place_of(pattern[0, slot], grid)] = slot


def ident_at(place, grid):
    rows, cols = grid
    row = lax.rem(lax.axis_index("row") + place // 3 - 1 + rows, jnp.int32(rows))
    col = lax.rem(lax.axis_index("col") + place % 3 - 1 + cols, jnp.int32(cols))
    return (row * cols + col).astype(F32)


def pair_at(low, high, grid):
    return jnp.where(on_left(1), ident_at(low, grid), ident_at(high, grid))


def is_live(idents, wanted):
    return jnp.max(jnp.where(idents == wanted, 1.0, 0.0), axis=0, keepdims=True) > 0


def tile_at(e):
    return slice(e * BLOCK, (e + 1) * BLOCK)


def fetch(sources, targets, sems):
    copies = [pltpu.make_async_copy(s, t, sems.at[i]) for i, (s, t) in enumerate(zip(sources, targets))]
    for copy in copies:
        copy.start()
    return copies


def fill_rest(message):
    if message.shape[0] > DEPTH:
        message[DEPTH:, :] = jnp.zeros((message.shape[0] - DEPTH, WIDE), F32)


def spread(which, slots, data, to_left, to_right, rows, table):
    first_half = on_left(HALF)
    rows[slots * HALF : (slots + 1) * HALF, :] = jnp.zeros((HALF, WIDE), F32)
    for step in range(HALF):
        rows[pl.ds(step, slots, stride=HALF), :] = data[:, step * WIDE : (step + 1) * WIDE]

    def block(place):
        own = rows[pl.ds(pl.multiple_of(table[which, place] * HALF, HALF), HALF), :]
        return own, swap(own)

    def tile(low, high):
        return (jnp.where(first_half, low[0], high[1]), jnp.where(first_half, low[1], high[0]))

    for e in range(3):
        a, b, c = block(3 * e), block(3 * e + 1), block(3 * e + 2)
        left, right = tile(a, b), tile(b, c)
        for part in range(2):
            to_left[pl.ds(e * BLOCK + part, HALF, stride=2), :] = left[part]
            to_right[pl.ds(e * BLOCK + part, HALF, stride=2), :] = right[part]
    fill_rest(to_left)
    fill_rest(to_right)


def spread_kernel(grid, slots, *refs):
    sources, (first_left, first_right, second_left, second_right, idents) = refs[:8], refs[8:13]
    patterns, datas, later, (rows, table, sems) = refs[13:15], refs[15:17], refs[17:21], refs[21:]
    copies = fetch(sources, (*patterns, *datas, *later), sems)
    for which, pattern in enumerate(patterns):
        copies[which].wait()
        note_slots(which, pattern, table, grid, slots)
    for which, pattern in enumerate(later):
        copies[4 + which].wait()
        for slot in range(slots):
            idents[which, slot : slot + 1, :] = jnp.full((1, WIDE), pattern[0, slot].astype(F32), F32)
    for which, pair in enumerate(((first_left, first_right), (second_left, second_right))):
        copies[2 + which].wait()
        spread(which, slots, datas[which], *pair, rows.at[which], table)


def is_even():
    return lax.rem(lax.axis_index("row"), 2) == 0


def ask_kernel(slots, first_left, first_right, second_left, second_right, idents, far, near):
    even = is_even()
    for which, (left, right) in enumerate(((first_left, first_right), (second_left, second_right))):
        at = which * ASK_ROWS
        last, following = left[tile_at(0)], left[tile_at(2)]
        near[at : at + BLOCK, :] = jnp.where(even, following, last)
        far[at : at + BLOCK, :] = jnp.where(even, last, following)
        last, following = fold(right[tile_at(0)]), fold(right[tile_at(2)])
        near[at + BLOCK : at + ASK_ROWS, :] = jnp.where(even, following, last)
        far[at + BLOCK : at + ASK_ROWS, :] = jnp.where(even, last, following)
        masks = 2 * ASK_ROWS + slots * which
        near[masks : masks + slots, :] = idents[which]
        far[masks : masks + slots, :] = idents[which]
    rest = 2 * (ASK_ROWS + slots)
    if near.shape[0] > rest:
        near[rest:, :] = jnp.zeros((near.shape[0] - rest, WIDE), F32)


def fold(right):
    return jnp.where(on_left(HALF), swap(right[:HALF]), right[HALF:])


def split(tile):
    high = tile.astype(BF16)
    return high, (tile - high.astype(F32)).astype(BF16)


def put_depth(factor, rows, tile):
    high, low = split(tile)
    for part, value in enumerate((high, low, high)):
        factor[rows, part * WIDE : (part + 1) * WIDE] = value


def fill_left_factor(at, left, right, factor):
    rows = tile_at(at)
    put_depth(factor.at[0], rows, left)
    put_depth(factor.at[1], rows, right)


def unfold(left, folded):
    first = on_left(HALF)
    other = jnp.concatenate([jnp.where(first, folded, swap(folded)), jnp.where(first, swap(folded), folded)], axis=0)
    return jnp.where(on_left(BLOCK), swap(left), other)


def fill_right_factor(own_left, own_right, from_left, from_right, factor):
    first = on_left(BLOCK)
    for e in range(3):
        at = pl.ds(e * WIDE, WIDE)
        near = jnp.where(first, 0.0, own_right[tile_at(e)])
        for side, pair in enumerate(((from_left[tile_at(e)], own_left[tile_at(e)]), (near, from_right[tile_at(e)]))):
            for k, tile in enumerate(pair):
                high, low = split(tile)
                for part, value in enumerate((high, high, low)):
                    factor[side, tile_at(2 * part + k), at] = value


def product(factor, by):
    return [
        lax.dot_general(factor[side], by[side], (((1,), (0,)), ((), ())), preferred_element_type=F32)
        for side in range(2)
    ]


def tiles_of(total, at, low, count):
    first = on_left(BLOCK)
    left, right = [], []
    for e in range(low, low + count):
        a, b = (side[tile_at(at), e * WIDE : (e + 1) * WIDE] for side in total)
        left.append(a + jnp.where(first, 0.0, swap(b)))
        right.append(b)
    return left, right


def put_all(total, first_out, second_out, sums, paired):
    shares = []
    for at, low in ((0, 0), (1, 1)):
        left, right = tiles_of(total, at, low, 2)
        shares.append((left[0], left[1], jnp.where(on_left(BLOCK), swap(right[0]), right[1])))
    even = is_even()
    for part, (last, following) in enumerate(zip(*shares)):
        if paired:
            last, following = jnp.where(even, last, following), jnp.where(even, following, last)
        first_out[tile_at(part), :] = last
        second_out[tile_at(part), :] = following
    left, right = tiles_of(total, 2, 0, 3)
    for e in range(3):
        sums[e] = left[e]
        sums[3 + e] = right[e]
    if paired:
        fill_rest(first_out)
        fill_rest(second_out)
        return
    for share, e in ((first_out, 0), (second_out, 2)):
        share[DEPTH : DEPTH + BLOCK, :] = left[e]
        share[DEPTH + BLOCK :, :] = fold(right[e])


def fill_own(left, right, factor):
    fill_left_factor(2, left[tile_at(1)], right[tile_at(1)], factor)


def fill_asked(which, grid, slots, asks, got, sent, factor):
    far, near = asks
    even = is_even()
    for at in range(2):
        from_far = even if at == 0 else jnp.logical_not(even)

        def asked(start, count):
            return jnp.where(from_far, far[start : start + count], near[start : start + count])

        if got is None:
            row = which * ASK_ROWS
            left, folded = asked(row, BLOCK), asked(row + BLOCK, HALF)
        else:
            pack = sent[at][WIDE:DEPTH]
            if at == 0:
                left, folded = sent[at][BLOCK:WIDE], fold(pack)
            else:
                left, folded = sent[at][:BLOCK], jnp.where(on_left(HALF), pack[:HALF], swap(pack[HALF:]))
            idents = asked(2 * ASK_ROWS + slots * which, slots)
            left = jnp.where(is_live(idents, pair_at(3, 4, grid)), left + got[at][DEPTH : DEPTH + BLOCK], 0.0)
            folded = jnp.where(is_live(idents, ident_at(5, grid)), folded + got[at][DEPTH + BLOCK :], 0.0)
        fill_left_factor(at, left, unfold(left, folded), factor)


def first_share_kernel(grid, slots, earlier, *refs):
    tiles, asks, refs = refs[:4], refs[4:6], refs[6:]
    got, sent = (refs[:2], refs[2:4]) if earlier else (None, None)
    to_last, to_next, sums, by, factor = refs[4 if earlier else 0 :]
    fill_right_factor(*tiles, by)
    fill_asked(0, grid, slots, asks, got, sent, factor)
    fill_own(tiles[0], tiles[1], factor)
    put_all(product(factor, by), to_last, to_next, sums, earlier)


def second_share_kernel(grid, slots, earlier, *refs):
    tiles, asks, refs = refs[:4], refs[4:6], refs[6:]
    got, sent = (refs[:2], refs[2:4]) if earlier else (None, None)
    first_by, first_factor, to_last, to_next, sums, by, factor = refs[4 if earlier else 0 :]
    fill_right_factor(*tiles, by)
    fill_asked(1, grid, slots, asks, got, sent, factor)
    fill_own(tiles[0], tiles[1], factor)
    both = [a + b for a, b in zip(product(factor, first_by), product(first_factor, by))]
    put_all(both, to_last, to_next, sums, earlier)


def total(sums, from_last, from_next):
    left = [sums[e] for e in range(3)]
    right = [sums[3 + e] for e in range(3)]
    for share, low in ((from_last, 0), (from_next, 1)):
        pack = share[WIDE:DEPTH]
        left[low] += share[:BLOCK]
        left[low + 1] += share[BLOCK:WIDE]
        right[low] += swap(pack)
        right[low + 1] += pack
    return left, right


def next_kernel(which, grid, idents, sums, from_last, from_next, to_left, to_right):
    first = on_left(BLOCK)
    left, right = total(sums, from_last, from_next)
    for e in range(3):
        keep_left = is_live(idents[which], pair_at(3 * e, 3 * e + 1, grid))
        keep_right = is_live(idents[which], pair_at(3 * e + 1, 3 * e + 2, grid))
        to_left[tile_at(e), :] = jnp.where(keep_left, left[e], 0.0)
        to_right[tile_at(e), :] = jnp.where(keep_right, jnp.where(first, swap(left[e]), right[e]), 0.0)
    fill_rest(to_left)
    fill_rest(to_right)


def final_kernel(which, grid, slots, idents, own_left, own_right, sums, far, near, _, out, dense, packed):
    first_half = on_left(HALF)
    even, odd = pl.ds(0, HALF, stride=2), pl.ds(1, HALF, stride=2)
    on_even = is_even()
    from_last = jnp.where(on_even, far[:DEPTH], near[:DEPTH])
    from_next = jnp.where(on_even, near[:DEPTH], far[:DEPTH])
    left, right = total(sums, from_last, from_next)
    for e in range(3):
        dense[e] = 2.0 * own_left[tile_at(e)] - left[e]
        dense[3 + e] = 2.0 * own_right[tile_at(e)] - right[e]
    for e in range(3):
        a, b = dense[e, even, :], dense[e, odd, :]
        packed[3 * e] = jnp.where(first_half, a, swap(b))
        packed[3 * e + 1] = jnp.where(first_half, swap(a), b)
        a, b = dense[3 + e, even, :], dense[3 + e, odd, :]
        packed[3 * e + 2] = jnp.where(first_half, swap(a), b)
    slot_holds = [idents[2 + which] == ident_at(place, grid) for place in range(9)]
    for step in range(HALF):
        line = jnp.zeros((slots, WIDE), F32)
        for place in range(9):
            line = jnp.where(slot_holds[place], packed[place, step : step + 1, :], line)
        out[:, step * WIDE : (step + 1) * WIDE] = line


def shift(block, axis, by):
    count = lax.axis_size(axis)
    return lax.ppermute(block, axis, [(i, (i + by) % count) for i in range(count)])


VM = pl.BlockSpec(memory_space=pltpu.VMEM)
HB = pl.BlockSpec(memory_space=pltpu.HBM)
PARAMS = pltpu.CompilerParams(vmem_limit_bytes=VMEM_LIMIT)


def stay(operand):
    return pltpu.with_memory_space_constraint(operand, pltpu.HBM)


def shape(*sizes):
    return jax.ShapeDtypeStruct(sizes, F32)


def call(kernel, out_shape, in_specs, out_specs, scratch, name, flops=0):
    return pl.pallas_call(
        kernel,
        out_shape=out_shape,
        in_specs=in_specs,
        out_specs=out_specs,
        scratch_shapes=scratch,
        compiler_params=PARAMS,
        cost_estimate=pl.CostEstimate(flops=flops, bytes_accessed=10**6, transcendentals=0),
        name=name,
    )


def tiles_shape(rest):
    return shape(DEPTH + rest, WIDE)


SHARES = tuple(tuple(shape(DEPTH + rest, WIDE) for rest in pair) for pair in SHARE_PADS)
LONG_SHARE = shape(DEPTH + ASK_ROWS, WIDE)
SUMS = shape(6, BLOCK, WIDE)
BY_SHAPE = (2, 3 * WIDE, 3 * WIDE)
FACTOR_SHAPE = (2, 3 * BLOCK, 3 * WIDE)


def call_all(kernel, outputs, operands, scratch, name):
    return call(kernel, outputs, [VM] * len(operands), [VM] * len(outputs), scratch, name)(*operands)


def along_col(to_left, to_right):
    return to_left, to_right, shift(to_right, "col", 1), shift(to_left, "col", -1)


def along_row(to_last, to_next):
    return shift(to_next, "row", 1), shift(to_last, "row", -1)


def in_pairs(far, near):
    rows = lax.axis_size("row")
    far = lax.ppermute(far, "row", [(i, (((i + 1) ^ 1) - 1) % rows) for i in range(rows)])
    return far, lax.ppermute(near, "row", [(i, i ^ 1) for i in range(rows)])


def shards(
    density,
    density_pattern,
    response,
    response_pattern,
    density_next_pattern,
    response_next_pattern,
    density_out_pattern,
    response_out_pattern,
):
    slots = density.shape[3]
    grid = (lax.axis_size("row"), lax.axis_size("col"))
    pattern_scratch = pltpu.SMEM((1, slots), jnp.int32)
    table = pltpu.SMEM((2, 16), jnp.int32)

    def flat(pattern):
        return stay(pattern.reshape(1, slots))

    def flat_data(data):
        return stay(data.reshape(slots, BLOCK * BLOCK))

    *tiles, idents = call(
        functools.partial(spread_kernel, grid, slots),
        [tiles_shape(r) for r in PADS[:4]] + [shape(4, slots, WIDE)],
        [HB] * 8,
        [VM] * 5,
        [pattern_scratch] * 2
        + [pltpu.VMEM((slots, BLOCK * BLOCK), F32)] * 2
        + [pattern_scratch] * 4
        + [pltpu.VMEM((2, (slots + 1) * HALF, WIDE), F32), table, pltpu.SemaphoreType.DMA((8,))],
        "spread",
    )(
        flat(density_pattern),
        flat(response_pattern),
        flat_data(density),
        flat_data(response),
        flat(density_next_pattern),
        flat(response_next_pattern),
        flat(density_out_pattern),
        flat(response_out_pattern),
    )

    def share(first, second, asks, shapes_of_share, earlier):
        first_outputs, second_outputs = ([*shapes, SUMS] for shapes in shapes_of_share)
        send = in_pairs if earlier else along_row
        factors = [jax.ShapeDtypeStruct(BY_SHAPE, BF16), jax.ShapeDtypeStruct(FACTOR_SHAPE, BF16)]
        scratch = [pltpu.VMEM(BY_SHAPE, BF16), pltpu.VMEM(FACTOR_SHAPE, BF16)]
        *first_sent, first_sums, first_by, first_factor = call_all(
            functools.partial(first_share_kernel, grid, slots, bool(earlier)),
            first_outputs + factors,
            (*first, *asks, *(earlier[0] if earlier else ())),
            [],
            "first_share",
        )
        first_got = send(*first_sent)
        *second_sent, second_sums = call_all(
            functools.partial(second_share_kernel, grid, slots, bool(earlier)),
            second_outputs,
            (*second, *asks, *(earlier[1] if earlier else ()), first_by, first_factor),
            scratch,
            "second_share",
        )
        second_got = send(*second_sent)
        return (first_sums, *first_got), (second_sums, *second_got), first_sent, second_sent

    first = along_col(*tiles[:2])
    asks = in_pairs(
        *call_all(
            functools.partial(ask_kernel, slots),
            [shape(2 * (ASK_ROWS + slots) + rest, WIDE) for rest in (0, NEAR_PAD)],
            (*tiles, idents),
            [],
            "ask",
        )
    )
    second = along_col(*tiles[2:])
    first_parts, second_parts, first_sent, second_sent = share(first, second, asks, ([LONG_SHARE] * 2,) * 2, ())
    earlier = ((*first_parts[1:], *first_sent), (*second_parts[1:], *second_sent))
    next_tiles = [
        call_all(
            functools.partial(next_kernel, which, grid),
            [tiles_shape(r) for r in PADS[4 + 2 * which : 6 + 2 * which]],
            (idents, *parts),
            [],
            name,
        )
        for which, parts, name in ((0, first_parts, "first_next"), (1, second_parts, "second_next"))
    ]
    first, second = along_col(*next_tiles[0]), along_col(*next_tiles[1])
    first_parts, second_parts, _, _ = share(first, second, asks, SHARES, earlier)

    def final_of(which, own, parts, earlier, name):
        scratch = [pltpu.VMEM((6, BLOCK, WIDE), F32), pltpu.VMEM((9, HALF, WIDE), F32)]
        kernel = functools.partial(final_kernel, which, grid, slots)
        return call(kernel, shape(slots, BLOCK * BLOCK), [VM] * 6 + [HB], VM, scratch, name)(
            idents, *own[:2], *parts, stay(earlier)
        )

    first_out = final_of(0, first, first_parts, flat_data(density), "first_final")
    second_out = final_of(1, second, second_parts, first_out, "second_final")
    return first_out.reshape(density.shape), second_out.reshape(density.shape)


def solution(mesh):
    data = P(("groups", "row"), "col", None, None, None)
    pattern = P(("groups", "row"), "col", None, None)
    return jax.shard_map(
        shards,
        mesh=mesh,
        in_specs=(data, pattern, data, pattern, pattern, pattern, pattern, pattern),
        out_specs=(data, data),
        check_vma=False,
    )
```

```python
import functools

import jax
import jax.numpy as jnp
from jax import lax
from jax.experimental import pallas as pl
from jax.experimental.pallas import tpu as pltpu
from jax.sharding import PartitionSpec as P

BLOCK = 64
WIDE = 2 * BLOCK
HALF = BLOCK // 2
DEPTH = 3 * BLOCK
ASK_ROWS = BLOCK + HALF
PADS = (16, 0, 0, 8, 8, 16, 0, 8)
NEAR_PAD = 8
SHARE_PADS = (8, 8), (0, 8)
LONG_PADS = (0, 8), (0, 8)
F32 = jnp.float32
BF16 = jnp.bfloat16
VMEM_LIMIT = 16 * 1024 * 1024


def on_left(rows):
    return lax.broadcasted_iota(jnp.int32, (rows, WIDE), 1) < BLOCK


def swap(tile):
    return pltpu.roll(tile, BLOCK, 1)


def place_of(ident, grid):
    rows, cols = grid
    source = jnp.maximum(ident, 0)
    owner_row = lax.div(source, jnp.int32(cols))
    owner_col = lax.rem(source, jnp.int32(cols))
    down = lax.rem(owner_row - lax.axis_index("row") + 1 + rows, jnp.int32(rows))
    across = lax.rem(owner_col - lax.axis_index("col") + 1 + cols, jnp.int32(cols))
    return jnp.where(ident < 0, 9, down * 3 + across)


def note_slots(which, pattern, table, grid, slots):
    for place in range(10):
        table[which, place] = slots
    for slot in range(slots):
        table[which, place_of(pattern[0, slot], grid)] = slot


def ident_at(place, grid):
    rows, cols = grid
    row = lax.rem(lax.axis_index("row") + place // 3 - 1 + rows, jnp.int32(rows))
    col = lax.rem(lax.axis_index("col") + place % 3 - 1 + cols, jnp.int32(cols))
    return (row * cols + col).astype(F32)


def pair_at(low, high, grid):
    return jnp.where(on_left(1), ident_at(low, grid), ident_at(high, grid))


def is_live(idents, wanted):
    return jnp.max(jnp.where(idents == wanted, 1.0, 0.0), axis=0, keepdims=True) > 0


def tile_at(e):
    return slice(e * BLOCK, (e + 1) * BLOCK)


def fetch(sources, targets, sems):
    copies = [pltpu.make_async_copy(s, t, sems.at[i]) for i, (s, t) in enumerate(zip(sources, targets))]
    for copy in copies:
        copy.start()
    return copies


def fill_rest(message):
    if message.shape[0] > DEPTH:
        message[DEPTH:, :] = jnp.zeros((message.shape[0] - DEPTH, WIDE), F32)


def spread(which, slots, data, to_left, to_right, rows, table):
    first_half = on_left(HALF)
    rows[slots * HALF : (slots + 1) * HALF, :] = jnp.zeros((HALF, WIDE), F32)
    for step in range(HALF):
        rows[pl.ds(step, slots, stride=HALF), :] = data[:, step * WIDE : (step + 1) * WIDE]

    def block(place):
        own = rows[pl.ds(pl.multiple_of(table[which, place] * HALF, HALF), HALF), :]
        return own, swap(own)

    def tile(low, high):
        return (jnp.where(first_half, low[0], high[1]), jnp.where(first_half, low[1], high[0]))

    for e in range(3):
        a, b, c = block(3 * e), block(3 * e + 1), block(3 * e + 2)
        left, right = tile(a, b), tile(b, c)
        for part in range(2):
            to_left[pl.ds(e * BLOCK + part, HALF, stride=2), :] = left[part]
            to_right[pl.ds(e * BLOCK + part, HALF, stride=2), :] = right[part]
    fill_rest(to_left)
    fill_rest(to_right)


def spread_kernel(grid, slots, *refs):
    sources, (first_left, first_right, second_left, second_right, idents) = refs[:8], refs[8:13]
    patterns, datas, later, (rows, table, sems) = refs[13:15], refs[15:17], refs[17:21], refs[21:]
    copies = fetch(sources, (*patterns, *datas, *later), sems)
    for which, pattern in enumerate(patterns):
        copies[which].wait()
        note_slots(which, pattern, table, grid, slots)
    for which, pattern in enumerate(later):
        copies[4 + which].wait()
        for slot in range(slots):
            idents[which, slot : slot + 1, :] = jnp.full((1, WIDE), pattern[0, slot].astype(F32), F32)
    for which, pair in enumerate(((first_left, first_right), (second_left, second_right))):
        copies[2 + which].wait()
        spread(which, slots, datas[which], *pair, rows.at[which], table)


def is_even():
    return lax.rem(lax.axis_index("row"), 2) == 0


def ask_kernel(slots, first_left, first_right, second_left, second_right, idents, far, near):
    even = is_even()
    for which, (left, right) in enumerate(((first_left, first_right), (second_left, second_right))):
        at = which * ASK_ROWS
        last, following = left[tile_at(0)], left[tile_at(2)]
        near[at : at + BLOCK, :] = jnp.where(even, following, last)
        far[at : at + BLOCK, :] = jnp.where(even, last, following)
        last, following = fold(right[tile_at(0)]), fold(right[tile_at(2)])
        near[at + BLOCK : at + ASK_ROWS, :] = jnp.where(even, following, last)
        far[at + BLOCK : at + ASK_ROWS, :] = jnp.where(even, last, following)
        masks = 2 * ASK_ROWS + slots * which
        near[masks : masks + slots, :] = idents[which]
        far[masks : masks + slots, :] = idents[which]
    rest = 2 * (ASK_ROWS + slots)
    if near.shape[0] > rest:
        near[rest:, :] = jnp.zeros((near.shape[0] - rest, WIDE), F32)


def fold(right):
    return jnp.where(on_left(HALF), swap(right[:HALF]), right[HALF:])


def split(tile):
    high = tile.astype(BF16)
    return high, (tile - high.astype(F32)).astype(BF16)


def put_depth(factor, rows, tile):
    high, low = split(tile)
    for part, value in enumerate((high, low, high)):
        factor[rows, part * WIDE : (part + 1) * WIDE] = value


def fill_left_factor(at, left, right, factor):
    rows = tile_at(at)
    put_depth(factor.at[0], rows, left)
    put_depth(factor.at[1], rows, right)


def unfold(left, folded):
    first = on_left(HALF)
    other = jnp.concatenate([jnp.where(first, folded, swap(folded)), jnp.where(first, swap(folded), folded)], axis=0)
    return jnp.where(on_left(BLOCK), swap(left), other)


def fill_right_factor(own_left, own_right, from_left, from_right, factor):
    first = on_left(BLOCK)
    for e in range(3):
        at = pl.ds(e * WIDE, WIDE)
        near = jnp.where(first, 0.0, own_right[tile_at(e)])
        for side, pair in enumerate(((from_left[tile_at(e)], own_left[tile_at(e)]), (near, from_right[tile_at(e)]))):
            for k, tile in enumerate(pair):
                high, low = split(tile)
                for part, value in enumerate((high, high, low)):
                    factor[side, tile_at(2 * part + k), at] = value


def product(factor, by):
    return [
        lax.dot_general(factor[side], by[side], (((1,), (0,)), ((), ())), preferred_element_type=F32)
        for side in range(2)
    ]


def tiles_of(total, at, low, count):
    first = on_left(BLOCK)
    left, right = [], []
    for e in range(low, low + count):
        a, b = (side[tile_at(at), e * WIDE : (e + 1) * WIDE] for side in total)
        left.append(a + jnp.where(first, 0.0, swap(b)))
        right.append(b)
    return left, right


def put_all(total, far, near, sums):
    even = is_even()

    def put(rows, last, following):
        far[rows, :] = jnp.where(even, last, following)
        near[rows, :] = jnp.where(even, following, last)

    shares = []
    for at, low in ((0, 0), (1, 1)):
        left, right = tiles_of(total, at, low, 2)
        shares.append((left[0], left[1], jnp.where(on_left(BLOCK), swap(right[0]), right[1])))
    for part, pair in enumerate(zip(*shares)):
        put(tile_at(part), *pair)
    left, right = tiles_of(total, 2, 0, 3)
    for e in range(3):
        sums[e] = left[e]
        sums[3 + e] = right[e]
    if far.shape[0] >= DEPTH + ASK_ROWS:
        put(slice(DEPTH, DEPTH + BLOCK), left[0], left[2])
        put(slice(DEPTH + BLOCK, DEPTH + ASK_ROWS), fold(right[0]), fold(right[2]))
    for message in (far, near):
        for length in (DEPTH, DEPTH + ASK_ROWS):
            if length < message.shape[0] < length + BLOCK:
                message[length:, :] = jnp.zeros((message.shape[0] - length, WIDE), F32)


def pick(pair, at, rows):
    far, near = pair
    even = is_even()
    return jnp.where(even if at == 0 else jnp.logical_not(even), far[rows], near[rows])


def fill_own(left, right, factor):
    fill_left_factor(2, left[tile_at(1)], right[tile_at(1)], factor)


def fill_asked(which, grid, slots, asks, got, sent, factor):
    far, near = asks
    even = is_even()
    for at in range(2):
        from_far = even if at == 0 else jnp.logical_not(even)

        def asked(start, count):
            return jnp.where(from_far, far[start : start + count], near[start : start + count])

        if got is None:
            row = which * ASK_ROWS
            left, folded = asked(row, BLOCK), asked(row + BLOCK, HALF)
        else:
            pack = pick(sent, at, slice(WIDE, DEPTH))
            outer, outer_fold = slice(DEPTH, DEPTH + BLOCK), slice(DEPTH + BLOCK, DEPTH + ASK_ROWS)
            if at == 0:
                left, folded = pick(sent, 0, slice(BLOCK, WIDE)), fold(pack)
            else:
                left, folded = pick(sent, 1, slice(0, BLOCK)), jnp.where(on_left(HALF), pack[:HALF], swap(pack[HALF:]))
            idents = asked(2 * ASK_ROWS + slots * which, slots)
            left = jnp.where(is_live(idents, pair_at(3, 4, grid)), left + pick(got, at, outer), 0.0)
            folded = jnp.where(is_live(idents, ident_at(5, grid)), folded + pick(got, at, outer_fold), 0.0)
        fill_left_factor(at, left, unfold(left, folded), factor)


def first_share_kernel(grid, slots, earlier, *refs):
    tiles, asks, refs = refs[:4], refs[4:6], refs[6:]
    got, sent = (refs[:2], refs[2:4]) if earlier else (None, None)
    to_last, to_next, sums, by, factor = refs[4 if earlier else 0 :]
    fill_right_factor(*tiles, by)
    fill_asked(0, grid, slots, asks, got, sent, factor)
    fill_own(tiles[0], tiles[1], factor)
    put_all(product(factor, by), to_last, to_next, sums)


def second_share_kernel(grid, slots, earlier, *refs):
    tiles, asks, refs = refs[:4], refs[4:6], refs[6:]
    got, sent = (refs[:2], refs[2:4]) if earlier else (None, None)
    first_by, first_factor, to_last, to_next, sums, by, factor = refs[4 if earlier else 0 :]
    fill_right_factor(*tiles, by)
    fill_asked(1, grid, slots, asks, got, sent, factor)
    fill_own(tiles[0], tiles[1], factor)
    both = [a + b for a, b in zip(product(factor, first_by), product(first_factor, by))]
    put_all(both, to_last, to_next, sums)


def total(sums, far, near):
    left = [sums[e] for e in range(3)]
    right = [sums[3 + e] for e in range(3)]
    for low in range(2):
        share = pick((far, near), low, slice(0, DEPTH))
        pack = share[WIDE:DEPTH]
        left[low] += share[:BLOCK]
        left[low + 1] += share[BLOCK:WIDE]
        right[low] += swap(pack)
        right[low + 1] += pack
    return left, right


def next_kernel(which, grid, idents, sums, far, near, to_left, to_right):
    first = on_left(BLOCK)
    left, right = total(sums, far, near)
    for e in range(3):
        keep_left = is_live(idents[which], pair_at(3 * e, 3 * e + 1, grid))
        keep_right = is_live(idents[which], pair_at(3 * e + 1, 3 * e + 2, grid))
        to_left[tile_at(e), :] = jnp.where(keep_left, left[e], 0.0)
        to_right[tile_at(e), :] = jnp.where(keep_right, jnp.where(first, swap(left[e]), right[e]), 0.0)
    fill_rest(to_left)
    fill_rest(to_right)


def final_kernel(which, grid, slots, idents, own_left, own_right, sums, far, near, _, out, dense, packed):
    first_half = on_left(HALF)
    even, odd = pl.ds(0, HALF, stride=2), pl.ds(1, HALF, stride=2)
    left, right = total(sums, far, near)
    for e in range(3):
        dense[e] = 2.0 * own_left[tile_at(e)] - left[e]
        dense[3 + e] = 2.0 * own_right[tile_at(e)] - right[e]
    for e in range(3):
        a, b = dense[e, even, :], dense[e, odd, :]
        packed[3 * e] = jnp.where(first_half, a, swap(b))
        packed[3 * e + 1] = jnp.where(first_half, swap(a), b)
        a, b = dense[3 + e, even, :], dense[3 + e, odd, :]
        packed[3 * e + 2] = jnp.where(first_half, swap(a), b)
    slot_holds = [idents[2 + which] == ident_at(place, grid) for place in range(9)]
    for step in range(HALF):
        line = jnp.zeros((slots, WIDE), F32)
        for place in range(9):
            line = jnp.where(slot_holds[place], packed[place, step : step + 1, :], line)
        out[:, step * WIDE : (step + 1) * WIDE] = line


def shift(block, axis, by):
    count = lax.axis_size(axis)
    return lax.ppermute(block, axis, [(i, (i + by) % count) for i in range(count)])


VM = pl.BlockSpec(memory_space=pltpu.VMEM)
HB = pl.BlockSpec(memory_space=pltpu.HBM)
PARAMS = pltpu.CompilerParams(vmem_limit_bytes=VMEM_LIMIT)


def stay(operand):
    return pltpu.with_memory_space_constraint(operand, pltpu.HBM)


def shape(*sizes):
    return jax.ShapeDtypeStruct(sizes, F32)


def call(kernel, out_shape, in_specs, out_specs, scratch, name, flops=0):
    return pl.pallas_call(
        kernel,
        out_shape=out_shape,
        in_specs=in_specs,
        out_specs=out_specs,
        scratch_shapes=scratch,
        compiler_params=PARAMS,
        cost_estimate=pl.CostEstimate(flops=flops, bytes_accessed=10**6, transcendentals=0),
        name=name,
    )


def tiles_shape(rest):
    return shape(DEPTH + rest, WIDE)


SHARES = tuple(tuple(shape(DEPTH + rest, WIDE) for rest in pair) for pair in SHARE_PADS)
LONG_SHARES = tuple(tuple(shape(DEPTH + ASK_ROWS + rest, WIDE) for rest in pair) for pair in LONG_PADS)
SUMS = shape(6, BLOCK, WIDE)
BY_SHAPE = (2, 3 * WIDE, 3 * WIDE)
FACTOR_SHAPE = (2, 3 * BLOCK, 3 * WIDE)


def call_all(kernel, outputs, operands, scratch, name):
    return call(kernel, outputs, [VM] * len(operands), [VM] * len(outputs), scratch, name)(*operands)


def along_col(to_left, to_right):
    return to_left, to_right, shift(to_right, "col", 1), shift(to_left, "col", -1)


def in_pairs(far, near):
    rows = lax.axis_size("row")
    far = lax.ppermute(far, "row", [(i, (((i + 1) ^ 1) - 1) % rows) for i in range(rows)])
    return far, lax.ppermute(near, "row", [(i, i ^ 1) for i in range(rows)])


def shards(
    density,
    density_pattern,
    response,
    response_pattern,
    density_next_pattern,
    response_next_pattern,
    density_out_pattern,
    response_out_pattern,
):
    slots = density.shape[3]
    grid = (lax.axis_size("row"), lax.axis_size("col"))
    pattern_scratch = pltpu.SMEM((1, slots), jnp.int32)
    table = pltpu.SMEM((2, 16), jnp.int32)

    def flat(pattern):
        return stay(pattern.reshape(1, slots))

    def flat_data(data):
        return stay(data.reshape(slots, BLOCK * BLOCK))

    *tiles, idents = call(
        functools.partial(spread_kernel, grid, slots),
        [tiles_shape(r) for r in PADS[:4]] + [shape(4, slots, WIDE)],
        [HB] * 8,
        [VM] * 5,
        [pattern_scratch] * 2
        + [pltpu.VMEM((slots, BLOCK * BLOCK), F32)] * 2
        + [pattern_scratch] * 4
        + [pltpu.VMEM((2, (slots + 1) * HALF, WIDE), F32), table, pltpu.SemaphoreType.DMA((8,))],
        "spread",
    )(
        flat(density_pattern),
        flat(response_pattern),
        flat_data(density),
        flat_data(response),
        flat(density_next_pattern),
        flat(response_next_pattern),
        flat(density_out_pattern),
        flat(response_out_pattern),
    )

    def share(first, second, asks, shapes_of_share, earlier):
        first_outputs, second_outputs = ([*shapes, SUMS] for shapes in shapes_of_share)
        factors = [jax.ShapeDtypeStruct(BY_SHAPE, BF16), jax.ShapeDtypeStruct(FACTOR_SHAPE, BF16)]
        scratch = [pltpu.VMEM(BY_SHAPE, BF16), pltpu.VMEM(FACTOR_SHAPE, BF16)]
        *first_sent, first_sums, first_by, first_factor = call_all(
            functools.partial(first_share_kernel, grid, slots, bool(earlier)),
            first_outputs + factors,
            (*first, *asks, *(earlier[0] if earlier else ())),
            [],
            "first_share",
        )
        first_got = in_pairs(*first_sent)
        *second_sent, second_sums = call_all(
            functools.partial(second_share_kernel, grid, slots, bool(earlier)),
            second_outputs,
            (*second, *asks, *(earlier[1] if earlier else ()), first_by, first_factor),
            scratch,
            "second_share",
        )
        second_got = in_pairs(*second_sent)
        return (first_sums, *first_got), (second_sums, *second_got), first_sent, second_sent

    first = along_col(*tiles[:2])
    asks = in_pairs(
        *call_all(
            functools.partial(ask_kernel, slots),
            [shape(2 * (ASK_ROWS + slots) + rest, WIDE) for rest in (0, NEAR_PAD)],
            (*tiles, idents),
            [],
            "ask",
        )
    )
    second = along_col(*tiles[2:])
    first_parts, second_parts, first_sent, second_sent = share(first, second, asks, LONG_SHARES, ())
    earlier = ((*first_parts[1:], *first_sent), (*second_parts[1:], *second_sent))
    next_tiles = [
        call_all(
            functools.partial(next_kernel, which, grid),
            [tiles_shape(r) for r in PADS[4 + 2 * which : 6 + 2 * which]],
            (idents, *parts),
            [],
            name,
        )
        for which, parts, name in ((0, first_parts, "first_next"), (1, second_parts, "second_next"))
    ]
    first, second = along_col(*next_tiles[0]), along_col(*next_tiles[1])
    first_parts, second_parts, _, _ = share(first, second, asks, SHARES, earlier)

    def final_of(which, own, parts, earlier, name):
        scratch = [pltpu.VMEM((6, BLOCK, WIDE), F32), pltpu.VMEM((9, HALF, WIDE), F32)]
        kernel = functools.partial(final_kernel, which, grid, slots)
        return call(kernel, shape(slots, BLOCK * BLOCK), [VM] * 6 + [HB], VM, scratch, name)(
            idents, *own[:2], *parts, stay(earlier)
        )

    first_out = final_of(0, first, first_parts, flat_data(density), "first_final")
    second_out = final_of(1, second, second_parts, first_out, "second_final")
    return first_out.reshape(density.shape), second_out.reshape(density.shape)


def solution(mesh):
    data = P(("groups", "row"), "col", None, None, None)
    pattern = P(("groups", "row"), "col", None, None)
    return jax.shard_map(
        shards,
        mesh=mesh,
        in_specs=(data, pattern, data, pattern, pattern, pattern, pattern, pattern),
        out_specs=(data, data),
        check_vma=False,
    )
```

```python
import functools

import jax
import jax.numpy as jnp
from jax import lax
from jax.experimental import pallas as pl
from jax.experimental.pallas import tpu as pltpu
from jax.sharding import PartitionSpec as P

BLOCK = 64
WIDE = 2 * BLOCK
HALF = BLOCK // 2
DEPTH = 3 * BLOCK
ASK_ROWS = BLOCK + HALF
PADS = (16, 0, 0, 8, 8, 16, 0, 8)
NEAR_PAD = 8
SHARE_PADS = (8, 8), (0, 8)
LONG_PADS = (0, 8), (0, 8)
F32 = jnp.float32
BF16 = jnp.bfloat16
VMEM_LIMIT = 16 * 1024 * 1024


def on_left(rows):
    return lax.broadcasted_iota(jnp.int32, (rows, WIDE), 1) < BLOCK


def swap(tile):
    return pltpu.roll(tile, BLOCK, 1)


def place_of(ident, grid):
    rows, cols = grid
    source = jnp.maximum(ident, 0)
    owner_row = lax.div(source, jnp.int32(cols))
    owner_col = lax.rem(source, jnp.int32(cols))
    down = lax.rem(owner_row - lax.axis_index("row") + 1 + rows, jnp.int32(rows))
    across = lax.rem(owner_col - lax.axis_index("col") + 1 + cols, jnp.int32(cols))
    return jnp.where(ident < 0, 9, down * 3 + across)


def note_slots(which, pattern, table, grid, slots):
    for place in range(10):
        table[which, place] = slots
    for slot in range(slots):
        table[which, place_of(pattern[0, slot], grid)] = slot


def ident_at(place, grid):
    rows, cols = grid
    row = lax.rem(lax.axis_index("row") + place // 3 - 1 + rows, jnp.int32(rows))
    col = lax.rem(lax.axis_index("col") + place % 3 - 1 + cols, jnp.int32(cols))
    return (row * cols + col).astype(F32)


def pair_at(low, high, grid):
    return jnp.where(on_left(1), ident_at(low, grid), ident_at(high, grid))


def is_live(idents, wanted):
    return jnp.max(jnp.where(idents == wanted, 1.0, 0.0), axis=0, keepdims=True) > 0


def tile_at(e):
    return slice(e * BLOCK, (e + 1) * BLOCK)


def fetch(sources, targets, sems):
    copies = [pltpu.make_async_copy(s, t, sems.at[i]) for i, (s, t) in enumerate(zip(sources, targets))]
    for copy in copies[2:4] + copies[:2] + copies[4:]:
        copy.start()
    return copies


def fill_rest(message):
    if message.shape[0] > DEPTH:
        message[DEPTH:, :] = jnp.zeros((message.shape[0] - DEPTH, WIDE), F32)


def spread(which, slots, data, to_left, to_right, rows, table):
    first_half = on_left(HALF)
    rows[slots * HALF : (slots + 1) * HALF, :] = jnp.zeros((HALF, WIDE), F32)
    for step in range(HALF):
        rows[pl.ds(step, slots, stride=HALF), :] = data[:, step * WIDE : (step + 1) * WIDE]

    def block(place):
        own = rows[pl.ds(pl.multiple_of(table[which, place] * HALF, HALF), HALF), :]
        return own, swap(own)

    def tile(low, high):
        return (jnp.where(first_half, low[0], high[1]), jnp.where(first_half, low[1], high[0]))

    for e in range(3):
        a, b, c = block(3 * e), block(3 * e + 1), block(3 * e + 2)
        left, right = tile(a, b), tile(b, c)
        for part in range(2):
            to_left[pl.ds(e * BLOCK + part, HALF, stride=2), :] = left[part]
            to_right[pl.ds(e * BLOCK + part, HALF, stride=2), :] = right[part]
    fill_rest(to_left)
    fill_rest(to_right)


def spread_kernel(grid, slots, *refs):
    sources, (first_left, first_right, second_left, second_right, idents) = refs[:8], refs[8:13]
    patterns, datas, later, (rows, table, sems) = refs[13:15], refs[15:17], refs[17:21], refs[21:]
    copies = fetch(sources, (*patterns, *datas, *later), sems)
    for which, pattern in enumerate(patterns):
        copies[which].wait()
        note_slots(which, pattern, table, grid, slots)
    for which, pattern in enumerate(later):
        copies[4 + which].wait()
        for slot in range(slots):
            idents[which, slot : slot + 1, :] = jnp.full((1, WIDE), pattern[0, slot].astype(F32), F32)
    for which, pair in enumerate(((first_left, first_right), (second_left, second_right))):
        copies[2 + which].wait()
        spread(which, slots, datas[which], *pair, rows.at[which], table)


def is_even():
    return lax.rem(lax.axis_index("row"), 2) == 0


def ask_kernel(slots, first_left, first_right, second_left, second_right, idents, far, near):
    even = is_even()
    for which, (left, right) in enumerate(((first_left, first_right), (second_left, second_right))):
        at = which * ASK_ROWS
        last, following = left[tile_at(0)], left[tile_at(2)]
        near[at : at + BLOCK, :] = jnp.where(even, following, last)
        far[at : at + BLOCK, :] = jnp.where(even, last, following)
        last, following = fold(right[tile_at(0)]), fold(right[tile_at(2)])
        near[at + BLOCK : at + ASK_ROWS, :] = jnp.where(even, following, last)
        far[at + BLOCK : at + ASK_ROWS, :] = jnp.where(even, last, following)
        masks = 2 * ASK_ROWS + slots * which
        near[masks : masks + slots, :] = idents[which]
        far[masks : masks + slots, :] = idents[which]
    rest = 2 * (ASK_ROWS + slots)
    if near.shape[0] > rest:
        near[rest:, :] = jnp.zeros((near.shape[0] - rest, WIDE), F32)


def fold(right):
    return jnp.where(on_left(HALF), swap(right[:HALF]), right[HALF:])


def split(tile):
    high = tile.astype(BF16)
    return high, (tile - high.astype(F32)).astype(BF16)


def put_depth(factor, rows, tile):
    high, low = split(tile)
    for part, value in enumerate((high, low, high)):
        factor[rows, part * WIDE : (part + 1) * WIDE] = value


def fill_left_factor(at, left, right, factor):
    rows = tile_at(at)
    put_depth(factor.at[0], rows, left)
    put_depth(factor.at[1], rows, right)


def unfold(left, folded):
    first = on_left(HALF)
    other = jnp.concatenate([jnp.where(first, folded, swap(folded)), jnp.where(first, swap(folded), folded)], axis=0)
    return jnp.where(on_left(BLOCK), swap(left), other)


def fill_right_factor(own_left, own_right, from_left, from_right, factor):
    first = on_left(BLOCK)
    for e in range(3):
        at = pl.ds(e * WIDE, WIDE)
        near = jnp.where(first, 0.0, own_right[tile_at(e)])
        for side, pair in enumerate(((from_left[tile_at(e)], own_left[tile_at(e)]), (near, from_right[tile_at(e)]))):
            for k, tile in enumerate(pair):
                high, low = split(tile)
                for part, value in enumerate((high, high, low)):
                    factor[side, tile_at(2 * part + k), at] = value


def product(factor, by):
    return [
        lax.dot_general(factor[side], by[side], (((1,), (0,)), ((), ())), preferred_element_type=F32)
        for side in range(2)
    ]


def tiles_of(total, at, low, count):
    first = on_left(BLOCK)
    left, right = [], []
    for e in range(low, low + count):
        a, b = (side[tile_at(at), e * WIDE : (e + 1) * WIDE] for side in total)
        left.append(a + jnp.where(first, 0.0, swap(b)))
        right.append(b)
    return left, right


def put_all(total, far, near, sums):
    even = is_even()

    def put(rows, last, following):
        far[rows, :] = jnp.where(even, last, following)
        near[rows, :] = jnp.where(even, following, last)

    shares = []
    for at, low in ((0, 0), (1, 1)):
        left, right = tiles_of(total, at, low, 2)
        shares.append((left[0], left[1], jnp.where(on_left(BLOCK), swap(right[0]), right[1])))
    for part, pair in enumerate(zip(*shares)):
        put(tile_at(part), *pair)
    left, right = tiles_of(total, 2, 0, 3)
    for e in range(3):
        sums[e] = left[e]
        sums[3 + e] = right[e]
    if far.shape[0] >= DEPTH + ASK_ROWS:
        put(slice(DEPTH, DEPTH + BLOCK), left[0], left[2])
        put(slice(DEPTH + BLOCK, DEPTH + ASK_ROWS), fold(right[0]), fold(right[2]))
    for message in (far, near):
        for length in (DEPTH, DEPTH + ASK_ROWS):
            if length < message.shape[0] < length + BLOCK:
                message[length:, :] = jnp.zeros((message.shape[0] - length, WIDE), F32)


def pick(pair, at, rows):
    far, near = pair
    even = is_even()
    return jnp.where(even if at == 0 else jnp.logical_not(even), far[rows], near[rows])


def fill_own(left, right, factor):
    fill_left_factor(2, left[tile_at(1)], right[tile_at(1)], factor)


def fill_asked(which, grid, slots, asks, got, sent, factor):
    far, near = asks
    even = is_even()
    for at in range(2):
        from_far = even if at == 0 else jnp.logical_not(even)

        def asked(start, count):
            return jnp.where(from_far, far[start : start + count], near[start : start + count])

        if got is None:
            row = which * ASK_ROWS
            left, folded = asked(row, BLOCK), asked(row + BLOCK, HALF)
        else:
            pack = pick(sent, at, slice(WIDE, DEPTH))
            outer, outer_fold = slice(DEPTH, DEPTH + BLOCK), slice(DEPTH + BLOCK, DEPTH + ASK_ROWS)
            if at == 0:
                left, folded = pick(sent, 0, slice(BLOCK, WIDE)), fold(pack)
            else:
                left, folded = pick(sent, 1, slice(0, BLOCK)), jnp.where(on_left(HALF), pack[:HALF], swap(pack[HALF:]))
            idents = asked(2 * ASK_ROWS + slots * which, slots)
            left = jnp.where(is_live(idents, pair_at(3, 4, grid)), left + pick(got, at, outer), 0.0)
            folded = jnp.where(is_live(idents, ident_at(5, grid)), folded + pick(got, at, outer_fold), 0.0)
        fill_left_factor(at, left, unfold(left, folded), factor)


def first_share_kernel(grid, slots, earlier, *refs):
    tiles, asks, refs = refs[:4], refs[4:6], refs[6:]
    got, sent = (refs[:2], refs[2:4]) if earlier else (None, None)
    to_last, to_next, sums, by, factor = refs[4 if earlier else 0 :]
    fill_right_factor(*tiles, by)
    fill_asked(0, grid, slots, asks, got, sent, factor)
    fill_own(tiles[0], tiles[1], factor)
    put_all(product(factor, by), to_last, to_next, sums)


def second_share_kernel(grid, slots, earlier, *refs):
    tiles, asks, refs = refs[:4], refs[4:6], refs[6:]
    got, sent = (refs[:2], refs[2:4]) if earlier else (None, None)
    first_by, first_factor, to_last, to_next, sums, by, factor = refs[4 if earlier else 0 :]
    fill_right_factor(*tiles, by)
    fill_asked(1, grid, slots, asks, got, sent, factor)
    fill_own(tiles[0], tiles[1], factor)
    both = [a + b for a, b in zip(product(factor, first_by), product(first_factor, by))]
    put_all(both, to_last, to_next, sums)


def total(sums, far, near):
    left = [sums[e] for e in range(3)]
    right = [sums[3 + e] for e in range(3)]
    for low in range(2):
        share = pick((far, near), low, slice(0, DEPTH))
        pack = share[WIDE:DEPTH]
        left[low] += share[:BLOCK]
        left[low + 1] += share[BLOCK:WIDE]
        right[low] += swap(pack)
        right[low + 1] += pack
    return left, right


def next_kernel(which, grid, idents, sums, far, near, to_left, to_right):
    first = on_left(BLOCK)
    left, right = total(sums, far, near)
    for e in range(3):
        keep_left = is_live(idents[which], pair_at(3 * e, 3 * e + 1, grid))
        keep_right = is_live(idents[which], pair_at(3 * e + 1, 3 * e + 2, grid))
        to_left[tile_at(e), :] = jnp.where(keep_left, left[e], 0.0)
        to_right[tile_at(e), :] = jnp.where(keep_right, jnp.where(first, swap(left[e]), right[e]), 0.0)
    fill_rest(to_left)
    fill_rest(to_right)


def final_kernel(which, grid, slots, idents, own_left, own_right, sums, far, near, _, out, dense, packed):
    first_half = on_left(HALF)
    even, odd = pl.ds(0, HALF, stride=2), pl.ds(1, HALF, stride=2)
    left, right = total(sums, far, near)
    for e in range(3):
        dense[e] = 2.0 * own_left[tile_at(e)] - left[e]
        dense[3 + e] = 2.0 * own_right[tile_at(e)] - right[e]
    for e in range(3):
        a, b = dense[e, even, :], dense[e, odd, :]
        packed[3 * e] = jnp.where(first_half, a, swap(b))
        packed[3 * e + 1] = jnp.where(first_half, swap(a), b)
        a, b = dense[3 + e, even, :], dense[3 + e, odd, :]
        packed[3 * e + 2] = jnp.where(first_half, swap(a), b)
    slot_holds = [idents[2 + which] == ident_at(place, grid) for place in range(9)]
    for step in range(HALF):
        line = jnp.zeros((slots, WIDE), F32)
        for place in range(9):
            line = jnp.where(slot_holds[place], packed[place, step : step + 1, :], line)
        out[:, step * WIDE : (step + 1) * WIDE] = line


def shift(block, axis, by):
    count = lax.axis_size(axis)
    return lax.ppermute(block, axis, [(i, (i + by) % count) for i in range(count)])


VM = pl.BlockSpec(memory_space=pltpu.VMEM)
HB = pl.BlockSpec(memory_space=pltpu.HBM)
PARAMS = pltpu.CompilerParams(vmem_limit_bytes=VMEM_LIMIT)


def stay(operand):
    return pltpu.with_memory_space_constraint(operand, pltpu.HBM)


def shape(*sizes):
    return jax.ShapeDtypeStruct(sizes, F32)


def call(kernel, out_shape, in_specs, out_specs, scratch, name, flops=0):
    return pl.pallas_call(
        kernel,
        out_shape=out_shape,
        in_specs=in_specs,
        out_specs=out_specs,
        scratch_shapes=scratch,
        compiler_params=PARAMS,
        cost_estimate=pl.CostEstimate(flops=flops, bytes_accessed=10**6, transcendentals=0),
        name=name,
    )


def tiles_shape(rest):
    return shape(DEPTH + rest, WIDE)


SHARES = tuple(tuple(shape(DEPTH + rest, WIDE) for rest in pair) for pair in SHARE_PADS)
LONG_SHARES = tuple(tuple(shape(DEPTH + ASK_ROWS + rest, WIDE) for rest in pair) for pair in LONG_PADS)
SUMS = shape(6, BLOCK, WIDE)
BY_SHAPE = (2, 3 * WIDE, 3 * WIDE)
FACTOR_SHAPE = (2, 3 * BLOCK, 3 * WIDE)


def call_all(kernel, outputs, operands, scratch, name):
    return call(kernel, outputs, [VM] * len(operands), [VM] * len(outputs), scratch, name)(*operands)


def along_col(to_left, to_right):
    return to_left, to_right, shift(to_right, "col", 1), shift(to_left, "col", -1)


def in_pairs(far, near):
    rows = lax.axis_size("row")
    far = lax.ppermute(far, "row", [(i, (((i + 1) ^ 1) - 1) % rows) for i in range(rows)])
    return far, lax.ppermute(near, "row", [(i, i ^ 1) for i in range(rows)])


def shards(
    density,
    density_pattern,
    response,
    response_pattern,
    density_next_pattern,
    response_next_pattern,
    density_out_pattern,
    response_out_pattern,
):
    slots = density.shape[3]
    grid = (lax.axis_size("row"), lax.axis_size("col"))
    pattern_scratch = pltpu.SMEM((1, slots), jnp.int32)
    table = pltpu.SMEM((2, 16), jnp.int32)

    def flat(pattern):
        return stay(pattern.reshape(1, slots))

    def flat_data(data):
        return stay(data.reshape(slots, BLOCK * BLOCK))

    *tiles, idents = call(
        functools.partial(spread_kernel, grid, slots),
        [tiles_shape(r) for r in PADS[:4]] + [shape(4, slots, WIDE)],
        [HB] * 8,
        [VM] * 5,
        [pattern_scratch] * 2
        + [pltpu.VMEM((slots, BLOCK * BLOCK), F32)] * 2
        + [pattern_scratch] * 4
        + [pltpu.VMEM((2, (slots + 1) * HALF, WIDE), F32), table, pltpu.SemaphoreType.DMA((8,))],
        "spread",
    )(
        flat(density_pattern),
        flat(response_pattern),
        flat_data(density),
        flat_data(response),
        flat(density_next_pattern),
        flat(response_next_pattern),
        flat(density_out_pattern),
        flat(response_out_pattern),
    )

    def share(first, second, asks, shapes_of_share, earlier):
        first_outputs, second_outputs = ([*shapes, SUMS] for shapes in shapes_of_share)
        factors = [jax.ShapeDtypeStruct(BY_SHAPE, BF16), jax.ShapeDtypeStruct(FACTOR_SHAPE, BF16)]
        scratch = [pltpu.VMEM(BY_SHAPE, BF16), pltpu.VMEM(FACTOR_SHAPE, BF16)]
        *first_sent, first_sums, first_by, first_factor = call_all(
            functools.partial(first_share_kernel, grid, slots, bool(earlier)),
            first_outputs + factors,
            (*first, *asks, *(earlier[0] if earlier else ())),
            [],
            "first_share",
        )
        first_got = in_pairs(*first_sent)
        *second_sent, second_sums = call_all(
            functools.partial(second_share_kernel, grid, slots, bool(earlier)),
            second_outputs,
            (*second, *asks, *(earlier[1] if earlier else ()), first_by, first_factor),
            scratch,
            "second_share",
        )
        second_got = in_pairs(*second_sent)
        return (first_sums, *first_got), (second_sums, *second_got), first_sent, second_sent

    first = along_col(*tiles[:2])
    asks = in_pairs(
        *call_all(
            functools.partial(ask_kernel, slots),
            [shape(2 * (ASK_ROWS + slots) + rest, WIDE) for rest in (0, NEAR_PAD)],
            (*tiles, idents),
            [],
            "ask",
        )
    )
    second = along_col(*tiles[2:])
    first_parts, second_parts, first_sent, second_sent = share(first, second, asks, LONG_SHARES, ())
    earlier = ((*first_parts[1:], *first_sent), (*second_parts[1:], *second_sent))
    next_tiles = [
        call_all(
            functools.partial(next_kernel, which, grid),
            [tiles_shape(r) for r in PADS[4 + 2 * which : 6 + 2 * which]],
            (idents, *parts),
            [],
            name,
        )
        for which, parts, name in ((0, first_parts, "first_next"), (1, second_parts, "second_next"))
    ]
    first, second = along_col(*next_tiles[0]), along_col(*next_tiles[1])
    first_parts, second_parts, _, _ = share(first, second, asks, SHARES, earlier)

    def final_of(which, own, parts, earlier, name):
        scratch = [pltpu.VMEM((6, BLOCK, WIDE), F32), pltpu.VMEM((9, HALF, WIDE), F32)]
        kernel = functools.partial(final_kernel, which, grid, slots)
        return call(kernel, shape(slots, BLOCK * BLOCK), [VM] * 6 + [HB], VM, scratch, name)(
            idents, *own[:2], *parts, stay(earlier)
        )

    first_out = final_of(0, first, first_parts, flat_data(density), "first_final")
    second_out = final_of(1, second, second_parts, first_out, "second_final")
    return first_out.reshape(density.shape), second_out.reshape(density.shape)


def solution(mesh):
    data = P(("groups", "row"), "col", None, None, None)
    pattern = P(("groups", "row"), "col", None, None)
    return jax.shard_map(
        shards,
        mesh=mesh,
        in_specs=(data, pattern, data, pattern, pattern, pattern, pattern, pattern),
        out_specs=(data, data),
        check_vma=False,
    )
```
